128 devices in a mesh: grp: 4 (over z_lo, core), ctx: 32 (over x, z_hi, y).
Axes of the slice: x: 4, y: 4, z: 4 (z_hi: 2, z_lo: 2; z = z_hi * 2 + z_lo), core: 2. Of those that a mesh axis runs over, the one named last changes fastest.
Arguments:
- patches: bfloat16 [4, 4096, 1024], P('grp', 'ctx'), may hold values from -6 to 6
- gain: float32 [1024], replicated, may hold values from 0.5 to 1.5
- w_qkv: bfloat16 [1024, 3072], replicated, as said below
- w_out: bfloat16 [1024, 1024], replicated, may hold values from -0.1875 to 0.1875
- image_ids: int32 [4, 4096], P('grp', 'ctx'), may hold values from 0 to 15, never falling along the last dimension, each value on 1 to 2048 neighbouring positions
- grad_out: bfloat16 [4, 4096, 1024], P('grp', 'ctx'), may hold values from -6 to 6
Outputs:
- out: bfloat16 [4, 4096, 1024], P('grp', 'ctx')
- grad_patches: bfloat16 [4, 4096, 1024], P('grp', 'ctx')
- grad_w_qkv: float32 [1024, 3072], P('ctx')
- grad_w_out: float32 [1024, 1024], P('ctx')
The draws below stay inside these ranges and needn't reach their ends.
Inputs may be any that keep to these rules, and one draw needn't show every extreme that they name: `image_ids`: along each sequence the ids never fall and take every value from 0 to 15; each image holds at most 2048 patches, and some image in every sequence draw holds exactly 2048. `w_qkv`: every entry lies within plus or minus 6 / sqrt(1024).
All inputs are finite; a program needn't handle non-finite values.
Results may differ from the reference program's by a relative error of at most 0.04.
Values may be sent and summed in bfloat16 or wider, within the bound.
No kernel may reach another device: no remote copies, remote signals or barrier semaphores. Data moves between devices by JAX's collectives and lax.ppermute only.
A program may use at most 256 MiB of HBM per device.

```python
import math
import jax
import jax.numpy as jnp
import numpy as np
from jax import lax

D = 1024
HEADS = 16
HEAD_DIM = 64
TOK_DEV = 128
SEQS = 4
SEQ = 4096
IMAGES = 16
IMG_MAX = 2048
N_CTX = 32


def draw_patches(key, part):
    own_key = jax.random.fold_in(key, 3)
    return jnp.clip(jax.random.normal(own_key, (SEQS, SEQ, D), jnp.float32), -6.0, 6.0).astype(jnp.bfloat16)


def draw_w_qkv(key, part):
    own_key = jax.random.fold_in(key, 5)
    limit = 6.0 / math.sqrt(D)
    base_key = jax.random.fold_in(own_key, 0)
    matrix = jax.random.normal(base_key, (D, 3 * D), jnp.float32) / math.sqrt(D)
    return jnp.clip(matrix, -limit, limit).astype(jnp.bfloat16)


def shard_levels(key, dims, cuts, low, top_value):
    factor_of, own = 1.0, jax.random.fold_in(key, 6)
    for position, shards_of in cuts:
        heights = jnp.exp(jax.random.uniform(jax.random.fold_in(own, position), (shards_of,), jnp.float32, low / len(cuts), top_value / len(cuts)))
        factor_of = factor_of * jnp.repeat(heights, dims[position] // shards_of).reshape([-1 if axis == position else 1 for axis in range(len(dims))])
    return factor_of


def split_up(number_of, total, most, slope):
    weights = [(1 << 20) // math.isqrt(rank ** slope) + 1 for rank in range(2, number_of + 1)]
    surplus, given = total - most - (number_of - 1), [1] * (number_of - 1)
    while surplus > 0:
        movable = [i for i in range(number_of - 1) if given[i] < most]
        whole, budget = sum([weights[i] for i in movable]), surplus
        for i in movable:
            more = min(most - given[i], max(1, budget * weights[i] // whole), surplus)
            given[i] = given[i] + more
            surplus = surplus - more
    return np.array([most] + given)


def uneven_parts(stream_key, count, total, most, skew):
    if count == 2:
        one = jax.random.randint(stream_key, (), max(1, total - most), min(most, total - 1) + 1)
        return jnp.stack([one, total - one])
    tallies = jnp.asarray(split_up(count, total, most, skew), jnp.int32)
    pairs = (count - 1) // 2
    giver, taker = tallies[1:1 + 2 * pairs:2], tallies[2:2 + 2 * pairs:2]
    slack = jnp.minimum(giver - 1, most - taker)
    shifted = jax.random.randint(jax.random.fold_in(stream_key, 1), (pairs,), 0, 1 << 20) % (slack + 1)
    tallies = tallies.at[1:1 + 2 * pairs:2].set(giver - shifted).at[2:2 + 2 * pairs:2].set(taker + shifted)
    return tallies[jax.random.permutation(jax.random.fold_in(stream_key, 2), count)]


def bell_draw(stream_key, extent, scale, most, shards=(), dtype=jnp.bfloat16):
    drawn = jax.random.normal(stream_key, extent, jnp.float32) * scale
    if len(shards) > 0:
        drawn = shard_levels(stream_key, extent, shards, -0.22, 0.18) * drawn
    return jnp.clip(drawn, min=-most, max=most).astype(dtype)


def setup_inputs(seed: int = 0) -> dict:
    key_list = jax.random.split(jax.random.key(seed), 7)
    return {
        "patches": draw_patches(jax.random.fold_in(key_list[6], 71), 0),
        "gain": jnp.clip(1.0 + 0.1 * jax.random.normal(key_list[1], (D,), jnp.float32), 0.5, 1.5),
        "w_qkv": draw_w_qkv(jax.random.fold_in(key_list[6], 71), 0),
        "w_out": bell_draw(key_list[3], (D, D), D ** -0.5, 0.1875),
        "image_ids": jax.vmap(lambda own: jnp.searchsorted(jnp.cumsum(uneven_parts(own, IMAGES, SEQ, IMG_MAX, 2)), jnp.arange(SEQ), side="right"))(jax.random.split(key_list[4], SEQS)).reshape((SEQS, SEQ)).astype(jnp.int32),
        "grad_out": bell_draw(key_list[5], (SEQS, SEQ, D), 1.0, 6.0, ((0, 4), (1, 32))),
    }


EPSILON = 1e-06
NEGATIVE = -1e+30

def head_terms(operands, matches):
    query_h, key_h, value_h, dattn_h = operands
    score_scale = 1.0 / math.sqrt(HEAD_DIM)
    scores = jnp.dot(query_h, key_h.T, preferred_element_type=jnp.float32) * score_scale
    masked = jnp.where(matches, scores, NEGATIVE)
    row_max = lax.optimization_barrier(jnp.max(masked, axis=1, keepdims=True))
    row_sum = lax.optimization_barrier(jnp.sum(jnp.where(matches, jnp.exp(masked - row_max), 0.0), axis=1, keepdims=True))
    log_total = row_max + jnp.log(row_sum)
    weights = jnp.where(matches, jnp.exp(masked - log_total), 0.0)
    rounded = weights.astype(jnp.bfloat16)
    output = jnp.dot(rounded, value_h, preferred_element_type=jnp.float32).astype(jnp.bfloat16)
    delta = lax.optimization_barrier(jnp.sum(dattn_h.astype(jnp.float32) * output.astype(jnp.float32), axis=1, keepdims=True))
    prob_grad = jnp.dot(dattn_h, value_h.T, preferred_element_type=jnp.float32)
    score_grad = (weights * (prob_grad - delta) * score_scale).astype(jnp.bfloat16)
    query_grad = jnp.dot(score_grad, key_h, preferred_element_type=jnp.float32)
    key_grad = jnp.dot(score_grad.T, query_h, preferred_element_type=jnp.float32)
    value_grad = jnp.dot(rounded.T, dattn_h, preferred_element_type=jnp.float32)
    return (output, query_grad, key_grad, value_grad)

def to_heads(block):
    return block.reshape(SEQ, HEADS, HEAD_DIM).transpose(1, 0, 2)

def from_heads(block):
    return block.transpose(1, 0, 2).reshape(SEQ, D)

def block_sum(left, right):
    left_blocks = left.reshape(N_CTX, TOK_DEV, left.shape[1])
    right_blocks = right.reshape(N_CTX, TOK_DEV, right.shape[1])

    def step(running, pair):
        term = jnp.dot(pair[0].T, pair[1], preferred_element_type=jnp.float32)
        term = lax.optimization_barrier(term.astype(jnp.bfloat16))
        return (running + term.astype(jnp.float32), None)
    start_sum = jnp.zeros((left.shape[1], right.shape[1]), jnp.float32)
    return lax.scan(step, start_sum, (left_blocks, right_blocks))[0]

def one_sequence(tokens, ident, cotangent, gain, w_qkv, w_out):
    values_f = tokens.astype(jnp.float32)
    average = lax.optimization_barrier(jnp.mean(values_f, axis=1, keepdims=True))
    centered = values_f - average
    variance = lax.optimization_barrier(jnp.mean(centered * centered, axis=1, keepdims=True))
    inv_std = lax.rsqrt(variance + EPSILON)
    x_hat = centered * inv_std
    normed = (x_hat * gain).astype(jnp.bfloat16)
    qkv = jnp.dot(normed, w_qkv, preferred_element_type=jnp.float32).astype(jnp.bfloat16)
    grad_attended = jnp.dot(cotangent, w_out.T, preferred_element_type=jnp.float32).astype(jnp.bfloat16)
    matches = ident[:, None] == ident[None, :]
    operands = (to_heads(qkv[:, :D]), to_heads(qkv[:, D:2 * D]), to_heads(qkv[:, 2 * D:]), to_heads(grad_attended))
    output, query_grad, key_grad, value_grad = lax.map(lambda item: head_terms(item, matches), operands)
    attended = from_heads(output)
    result = jnp.dot(attended, w_out, preferred_element_type=jnp.float32).astype(jnp.bfloat16)
    grad_qkv = jnp.concatenate([from_heads(query_grad), from_heads(key_grad), from_heads(value_grad)], axis=1).astype(jnp.bfloat16)
    grad_normed = jnp.dot(grad_qkv, w_qkv.T, preferred_element_type=jnp.float32) * gain
    grad_tokens = inv_std * (grad_normed - lax.optimization_barrier(jnp.mean(grad_normed, axis=1, keepdims=True)) - x_hat * lax.optimization_barrier(jnp.mean(grad_normed * x_hat, axis=1, keepdims=True)))
    return (result, grad_tokens.astype(jnp.bfloat16), block_sum(normed, grad_qkv), block_sum(attended, cotangent))

def reference(patches, gain, w_qkv, w_out, image_ids, grad_out):
    results = []
    grads = []
    qkv_total = jnp.zeros((D, 3 * D), jnp.float32)
    out_total = jnp.zeros((D, D), jnp.float32)
    for index in range(SEQS):
        result, grad_tokens, qkv_part, out_part = one_sequence(patches[index], image_ids[index], grad_out[index], gain, w_qkv, w_out)
        results.append(result)
        grads.append(grad_tokens)
        qkv_total = qkv_total + qkv_part
        out_total = out_total + out_part
    factor = 1.0 / math.sqrt(SEQS * SEQ)
    return (jnp.stack(results), jnp.stack(grads), qkv_total * factor, out_total * factor)
```

```python
import functools
import math

import jax
import jax.numpy as jnp
from jax import lax
from jax.experimental import pallas as pl
from jax.experimental.pallas import tpu as pltpu
from jax.sharding import PartitionSpec as P

HEADS = 16
HEAD_DIM = 64
D = HEADS * HEAD_DIM
TOK = 128
HALF = TOK // 2
N_CTX = 32
N_GRP = 4
SEQ = TOK * N_CTX
ID_ROWS = 16
IN_ROWS = TOK + HALF + ID_ROWS
OUT_ROWS = TOK + HALF
TQ = 256
TK = 512
Q_SRC = TQ // HALF
N_QB = N_CTX // Q_SRC
EPSILON = 1e-06
MASK = -1e30
VMEM = 56 * 1024 * 1024
F32 = jnp.float32
BF16 = jnp.bfloat16


def dot_nn(a, b):
    return jnp.dot(a, b, preferred_element_type=F32)


def dot_nt(a, b):
    return lax.dot_general(a, b, (((1,), (1,)), ((), ())), preferred_element_type=F32)


def dot_tn(a, b):
    return lax.dot_general(a, b, (((0,), (0,)), ((), ())), preferred_element_type=F32)


def lanes(shape):
    return lax.broadcasted_iota(jnp.int32, shape, 1)


def project_kernel(x_ref, cot_ref, gain_ref, ids_ref, wq_ref, wk_ref, wv_ref, wo_ref, send_ref, normed_ref):
    @pl.when(pl.program_id(0) == 0)
    def _():
        x = x_ref[...].astype(F32)
        cen = x - jnp.mean(x, axis=1, keepdims=True)
        inv = lax.rsqrt(jnp.mean(cen * cen, axis=1, keepdims=True) + EPSILON)
        normed_ref[...] = (cen * inv * gain_ref[...]).astype(BF16)

    n = normed_ref[...]
    q = dot_nn(n, wq_ref[...])
    k = dot_nn(n, wk_ref[...])
    v = dot_nn(n, wv_ref[...])
    g = dot_nt(cot_ref[...], wo_ref[...])
    ids = ids_ref[...].astype(F32)
    rolled = jnp.concatenate([ids[:, HALF:], ids[:, :HALF]], axis=1)
    for h in range(4):
        cols = slice(h * HEAD_DIM, (h + 1) * HEAD_DIM)
        kv = jnp.concatenate([k[:, cols], v[:, cols]], axis=1).astype(BF16)
        qg = jnp.concatenate([q[:, cols], g[:, cols]], axis=1).astype(BF16)
        for p in range(2):
            own = ids if p == 0 else rolled
            rows = jnp.concatenate(
                [jnp.broadcast_to(ids, (8, TOK)), jnp.broadcast_to(own, (8, TOK))], axis=0
            )
            send_ref[2 * h + p, :TOK, :] = kv
            send_ref[2 * h + p, TOK:OUT_ROWS, :] = qg[p * HALF:(p + 1) * HALF, :]
            send_ref[2 * h + p, OUT_ROWS:, :] = rows.astype(BF16)


def project(x, cot, gain, ids, w_qkv, w_out):
    whole = lambda shape: pl.BlockSpec(shape, lambda j: (0, 0))
    return pl.pallas_call(
        project_kernel,
        grid=(4,),
        in_specs=[
            whole((TOK, D)),
            whole((TOK, D)),
            whole((1, D)),
            whole((1, TOK)),
            pl.BlockSpec((D, 256), lambda j: (0, j)),
            pl.BlockSpec((D, 256), lambda j: (0, 4 + j)),
            pl.BlockSpec((D, 256), lambda j: (0, 8 + j)),
            pl.BlockSpec((256, D), lambda j: (j, 0)),
        ],
        out_specs=[pl.BlockSpec((8, IN_ROWS, TOK), lambda j: (j, 0, 0)), whole((TOK, D))],
        out_shape=[
            jax.ShapeDtypeStruct((N_CTX, IN_ROWS, TOK), BF16),
            jax.ShapeDtypeStruct((TOK, D), BF16),
        ],
        compiler_params=pltpu.CompilerParams(vmem_limit_bytes=VMEM),
        name="project",
    )(x, cot, gain, ids, w_qkv, w_qkv, w_qkv, w_out)


def attend_kernel(recv_ref, send_ref, kx, kvt, idm, sc, acc):
    lane = lanes((TOK, TOK))

    def prepare(c, carry):
        kv = recv_ref[c, :TOK, :].astype(F32)
        idrow = recv_ref[c, OUT_ROWS:, :].astype(F32)[:1]
        idm[pl.ds(c, 1), :] = idrow
        idcol = jnp.broadcast_to(idrow, (TOK, TOK)).T
        onehot = jnp.where(lane.astype(F32) - HEAD_DIM == idcol, 1.0, 0.0)
        rows = pl.ds(pl.multiple_of(c * TOK, TOK), TOK)
        kx[rows, :] = jnp.where(lane < HEAD_DIM, kv, onehot).astype(BF16)
        kvt[:, rows] = kv.T.astype(BF16)
        acc[rows, :] = jnp.zeros((TOK, TOK), F32)
        return carry

    lax.fori_loop(0, N_CTX, prepare, 0, unroll=4)

    lane_q = lanes((TQ, TOK))

    def fold(tile, op):
        out = tile[0:8]
        for r in range(8, tile.shape[0], 8):
            out = op(out, tile[r:r + 8])
        return out

    def query_block(i, carry):
        c0 = i * Q_SRC
        qd = recv_ref[pl.ds(c0, Q_SRC), TOK:OUT_ROWS, :].reshape(TQ, TOK).astype(F32)
        idcols = []
        lowest, highest = None, None
        for a in range(Q_SRC):
            both = recv_ref[c0 + a, OUT_ROWS:, :].astype(F32)
            idcols.append(jnp.broadcast_to(both[8:9], (TOK, TOK)).T[:HALF])
            lowest = both if lowest is None else jnp.minimum(lowest, both)
            highest = both if highest is None else jnp.maximum(highest, both)
        idcol = jnp.concatenate(idcols, axis=0)
        every = idm[...]
        below = jnp.sum(jnp.where(every < jnp.min(lowest), 1.0, 0.0)).astype(jnp.int32)
        upto = jnp.sum(jnp.where(every <= jnp.max(highest), 1.0, 0.0)).astype(jnp.int32)
        first = below // TK
        last = (upto + (TK - 1)) // TK

        other = jnp.where(
            (lane_q < HEAD_DIM + HEADS) & (lane_q.astype(F32) - HEAD_DIM != idcol), MASK, 0.0
        )
        qx = jnp.where(lane_q < HEAD_DIM, qd * 0.125, other)
        qxt = qx.T.astype(BF16)
        gz = jnp.where(lane_q >= HEAD_DIM, qd, 0.0)
        gzt_f = gz.T
        gzt = gzt_f.astype(BF16)

        def at(kb):
            return pl.ds(pl.multiple_of(kb * TK, TK), TK)

        def score_step(kb, top):
            s = dot_nn(kx[at(kb), :], qxt)
            sc[at(kb), :] = s
            return jnp.maximum(top, fold(s, jnp.maximum))

        top = lax.fori_loop(first, last, score_step, jnp.full((8, TQ), MASK, F32))
        top = jnp.max(top, axis=0, keepdims=True)

        def value_step(kb, state):
            total, ot = state
            e = jnp.exp(sc[at(kb), :] - top)
            sc[at(kb), :] = e
            return (
                total + fold(e, jnp.add),
                ot + dot_nn(kvt[HEAD_DIM:, at(kb)], e.astype(BF16)),
            )

        total, ot = lax.fori_loop(
            first, last, value_step, (jnp.zeros((8, TQ), F32), jnp.zeros((HEAD_DIM, TQ), F32))
        )
        inv = 1.0 / jnp.sum(total, axis=0, keepdims=True)
        ot = (ot * inv).astype(BF16).astype(F32)
        delta = jnp.sum(ot * gzt_f[HEAD_DIM:], axis=0, keepdims=True)

        scaled = (qd.T * inv).T
        right_q = jnp.where(lane_q < HEAD_DIM, scaled * 0.125, 0.0).astype(BF16)
        right_g = jnp.where(lane_q >= HEAD_DIM, scaled, 0.0).astype(BF16)

        def grad_step(kb, dqt):
            rows = recv_ref[pl.ds(kb * (TK // TOK), TK // TOK), :TOK, :].reshape(TK, TOK)
            dp = dot_nn(rows, gzt)
            e = sc[at(kb), :]
            ds = (e * (dp - delta)).astype(BF16)
            acc[at(kb), :] += dot_nn(ds, right_q) + dot_nn(e.astype(BF16), right_g)
            return dqt + dot_nn(kvt[:HEAD_DIM, at(kb)], ds)

        dqt = lax.fori_loop(first, last, grad_step, jnp.zeros((HEAD_DIM, TQ), F32))
        both = jnp.concatenate([ot, dqt * (inv * 0.125)], axis=0).T.astype(BF16)
        for a in range(Q_SRC):
            send_ref[c0 + a, TOK:, :] = both[a * HALF:(a + 1) * HALF]
        return carry

    lax.fori_loop(0, N_QB, query_block, 0)

    def finish(c, carry):
        rows = pl.ds(pl.multiple_of(c * TOK, TOK), TOK)
        send_ref[c, :TOK, :] = acc[rows, :].astype(BF16)
        return carry

    lax.fori_loop(0, N_CTX, finish, 0, unroll=4)


def attend(recv):
    vmem = pl.BlockSpec(memory_space=pltpu.VMEM)
    return pl.pallas_call(
        attend_kernel,
        in_specs=[vmem],
        out_specs=vmem,
        out_shape=jax.ShapeDtypeStruct((N_CTX, OUT_ROWS, TOK), BF16),
        scratch_shapes=[
            pltpu.VMEM((SEQ, TOK), BF16),
            pltpu.VMEM((TOK, SEQ), BF16),
            pltpu.VMEM((N_CTX, TOK), F32),
            pltpu.VMEM((SEQ, TQ), F32),
            pltpu.VMEM((SEQ, TOK), F32),
        ],
        compiler_params=pltpu.CompilerParams(vmem_limit_bytes=VMEM),
        name="attend",
    )(recv)


def unproject_kernel(recv_ref, x_ref, gain_ref, wq_ref, wk_ref, wv_ref, wo_ref, out_ref, gx_ref, cols_ref, sum_out, sum_g, sum_sel):
    step = pl.program_id(0)

    @pl.when(step == 0)
    def _():
        sum_out[...] = jnp.zeros_like(sum_out)
        sum_g[...] = jnp.zeros_like(sum_g)
        sum_sel[...] = jnp.zeros_like(sum_sel)

    att, dq, dk, dv = [], [], [], []
    for h in range(4):
        lo, hi = recv_ref[2 * h].astype(F32), recv_ref[2 * h + 1].astype(F32)
        kv = lo[:TOK] + hi[:TOK]
        aq = jnp.concatenate([lo[TOK:], hi[TOK:]], axis=0)
        att.append(aq[:, :HEAD_DIM])
        dq.append(aq[:, HEAD_DIM:])
        dk.append(kv[:, :HEAD_DIM])
        dv.append(kv[:, HEAD_DIM:])
    att, dq, dk, dv = [jnp.concatenate(t, axis=1).astype(BF16) for t in (att, dq, dk, dv)]

    row = lax.broadcasted_iota(jnp.int32, (256, D), 0) + step * 256
    place = ((row % 32) // 8) * 256 + (row // 32) * 8 + row % 8
    chosen = jnp.where(lanes((256, D)) == place, 1.0, 0.0).astype(BF16)
    sum_sel[...] += dot_nn(att, chosen)
    sum_out[...] += dot_nn(att, wo_ref[...])
    sum_g[...] += dot_nt(dq, wq_ref[...]) + dot_nt(dk, wk_ref[...]) + dot_nt(dv, wv_ref[...])
    cols_ref[step, :, :256] = dq
    cols_ref[step, :, 256:512] = dk
    cols_ref[step, :, 512:768] = dv

    @pl.when(step == 3)
    def _():
        out_ref[...] = sum_out[...].astype(BF16)
        for j in range(N_GRP):
            cols_ref[j, :, 768:] = sum_sel[:, j * 256:(j + 1) * 256].astype(BF16)
        x = x_ref[...].astype(F32)
        cen = x - jnp.mean(x, axis=1, keepdims=True)
        inv = lax.rsqrt(jnp.mean(cen * cen, axis=1, keepdims=True) + EPSILON)
        x_hat = cen * inv
        g = sum_g[...] * gain_ref[...]
        gx = inv * (
            g - jnp.mean(g, axis=1, keepdims=True) - x_hat * jnp.mean(g * x_hat, axis=1, keepdims=True)
        )
        gx_ref[...] = gx.astype(BF16)


def unproject(recv, x, gain, w_qkv, w_out):
    whole = lambda shape: pl.BlockSpec(shape, lambda j: (0,) * len(shape))
    return pl.pallas_call(
        unproject_kernel,
        grid=(4,),
        in_specs=[
            pl.BlockSpec((8, OUT_ROWS, TOK), lambda j: (j, 0, 0)),
            whole((TOK, D)),
            whole((1, D)),
            pl.BlockSpec((D, 256), lambda j: (0, j)),
            pl.BlockSpec((D, 256), lambda j: (0, 4 + j)),
            pl.BlockSpec((D, 256), lambda j: (0, 8 + j)),
            pl.BlockSpec((256, D), lambda j: (j, 0)),
        ],
        out_specs=[whole((TOK, D)), whole((TOK, D)), whole((N_GRP, TOK, D))],
        out_shape=[
            jax.ShapeDtypeStruct((TOK, D), BF16),
            jax.ShapeDtypeStruct((TOK, D), BF16),
            jax.ShapeDtypeStruct((N_GRP, TOK, D), BF16),
        ],
        scratch_shapes=[pltpu.VMEM((TOK, D), F32)] * 3,
        compiler_params=pltpu.CompilerParams(vmem_limit_bytes=VMEM),
        name="unproject",
    )(recv, x, gain, w_qkv, w_qkv, w_qkv, w_out)


def weights_kernel(both_ref, cols_ref, send_ref):
    both = both_ref[...].reshape(N_GRP * TOK, 2 * D)
    cols = cols_ref[...].reshape(N_GRP * TOK, D)
    for m in range(4):
        part = dot_tn(both[:, m * 256:(m + 1) * 256], cols[:, :768])
        for c in range(8):
            send_ref[8 * m + c, :, :768] = part[32 * c:32 * c + 32].astype(BF16)
    part = dot_tn(cols[:, 768:], both[:, D:])
    for c in range(N_CTX):
        rows = part[8 * c:8 * c + 8]
        piece = jnp.concatenate([rows[:, q * 256:(q + 1) * 256] for q in range(4)], axis=0)
        send_ref[c, :, 768:] = piece.astype(BF16)


def weights(both, cols):
    vmem = pl.BlockSpec(memory_space=pltpu.VMEM)
    return pl.pallas_call(
        weights_kernel,
        in_specs=[vmem, vmem],
        out_specs=vmem,
        out_shape=jax.ShapeDtypeStruct((N_CTX, 32, D), BF16),
        compiler_params=pltpu.CompilerParams(vmem_limit_bytes=VMEM),
        name="weights",
    )(both, cols)


def shards(patches, gain, w_qkv, w_out, image_ids, grad_out):
    x, cot = patches[0], grad_out[0]
    gain_row = gain[None]
    send, normed = project(x, cot, gain_row, image_ids, w_qkv, w_out)
    recv = lax.all_to_all(send, "ctx", 0, 0, tiled=True)
    both = lax.all_gather(jnp.concatenate([normed, cot], axis=1), "grp", axis=0)
    back = lax.all_to_all(attend(recv), "ctx", 0, 0, tiled=True)
    out, grad_x, cols = unproject(back, x, gain_row, w_qkv, w_out)
    cols = lax.all_to_all(cols, "grp", 0, 0, tiled=True)
    parts = lax.all_to_all(weights(both, cols), "ctx", 0, 0, tiled=True)
    factor = 1.0 / math.sqrt(N_GRP * SEQ)
    share = (jnp.sum(parts.astype(F32), axis=0) * factor).astype(BF16)
    full = lax.all_gather(share, "grp", axis=0).astype(F32)
    grad_qkv = full[:, :, :768].reshape(N_GRP, 32, 3, 256).transpose(1, 2, 0, 3).reshape(32, 3 * D)
    grad_out_w = full[:, :, 768:].reshape(N_GRP, 4, 8, 256).transpose(0, 2, 1, 3).reshape(32, D)
    return out[None], grad_x[None], grad_qkv, grad_out_w


def solution(mesh):
    in_specs = (P("grp", "ctx", None), P(), P(), P(), P("grp", "ctx"), P("grp", "ctx", None))
    out_specs = (P("grp", "ctx", None), P("grp", "ctx", None), P("ctx", None), P("ctx", None))
    return jax.shard_map(shards, mesh=mesh, in_specs=in_specs, out_specs=out_specs, check_vma=False)
```

```python
import functools
import math

import jax
import jax.numpy as jnp
from jax import lax
from jax.experimental import pallas as pl
from jax.experimental.pallas import tpu as pltpu
from jax.sharding import Mesh, PartitionSpec as P

HEADS = 16
HEAD_DIM = 64
D = HEADS * HEAD_DIM
TOK = 128
HALF = TOK // 2
N_CTX = 32
N_GRP = 4
N_X = 4
N_R = 8
SEQ = TOK * N_CTX
ID_ROWS = 16
IN_ROWS = TOK + HALF + ID_ROWS
OUT_ROWS = TOK + HALF
TQ = 256
TK = 1152
SUB = 128
Q_SRC = TQ // HALF
N_QB = N_CTX // Q_SRC
EPSILON = 1e-06
MASK = -1e30
VMEM = 56 * 1024 * 1024
F32 = jnp.float32
BF16 = jnp.bfloat16


def dot_nn(a, b):
    return jnp.dot(a, b, preferred_element_type=F32)


def dot_nt(a, b):
    return lax.dot_general(a, b, (((1,), (1,)), ((), ())), preferred_element_type=F32)


def dot_tn(a, b):
    return lax.dot_general(a, b, (((0,), (0,)), ((), ())), preferred_element_type=F32)


def lanes(shape):
    return lax.broadcasted_iota(jnp.int32, shape, 1)


def project_kernel(x_ref, cot_ref, gain_ref, ids_ref, wq_ref, wk_ref, wv_ref, wo_ref, send_ref, both_ref):
    @pl.when(pl.program_id(0) == 0)
    def _():
        x = x_ref[...].astype(F32)
        cen = x - jnp.mean(x, axis=1, keepdims=True)
        inv = lax.rsqrt(jnp.mean(cen * cen, axis=1, keepdims=True) + EPSILON)
        both_ref[:, :D] = (cen * inv * gain_ref[...]).astype(BF16)
        both_ref[:, D:] = cot_ref[...]

    n = both_ref[:, :D]
    q = dot_nn(n, wq_ref[...])
    k = dot_nn(n, wk_ref[...])
    v = dot_nn(n, wv_ref[...])
    g = dot_nt(cot_ref[...], wo_ref[...])
    ids = ids_ref[...].astype(F32)
    rolled = jnp.concatenate([ids[:, HALF:], ids[:, :HALF]], axis=1)
    for h in range(4):
        cols = slice(h * HEAD_DIM, (h + 1) * HEAD_DIM)
        kv = jnp.concatenate([k[:, cols], v[:, cols]], axis=1).astype(BF16)
        qg = jnp.concatenate([q[:, cols], g[:, cols]], axis=1).astype(BF16)
        for p in range(2):
            own = ids if p == 0 else rolled
            rows = jnp.concatenate(
                [jnp.broadcast_to(ids, (8, TOK)), jnp.broadcast_to(own, (8, TOK))], axis=0
            )
            send_ref[2 * h + p, :TOK, :] = kv
            send_ref[2 * h + p, TOK:OUT_ROWS, :] = qg[p * HALF:(p + 1) * HALF, :]
            send_ref[2 * h + p, OUT_ROWS:, :] = rows.astype(BF16)


def project(x, cot, gain, ids, w_qkv, w_out):
    whole = lambda shape: pl.BlockSpec(shape, lambda j: (0, 0))
    return pl.pallas_call(
        project_kernel,
        grid=(4,),
        in_specs=[
            whole((TOK, D)),
            whole((TOK, D)),
            whole((1, D)),
            whole((1, TOK)),
            pl.BlockSpec((D, 256), lambda j: (0, j)),
            pl.BlockSpec((D, 256), lambda j: (0, 4 + j)),
            pl.BlockSpec((D, 256), lambda j: (0, 8 + j)),
            pl.BlockSpec((256, D), lambda j: (j, 0)),
        ],
        out_specs=[pl.BlockSpec((8, IN_ROWS, TOK), lambda j: (j, 0, 0)), whole((TOK, 2 * D))],
        out_shape=[
            jax.ShapeDtypeStruct((N_CTX, IN_ROWS, TOK), BF16),
            jax.ShapeDtypeStruct((TOK, 2 * D), BF16),
        ],
        compiler_params=pltpu.CompilerParams(vmem_limit_bytes=VMEM),
        name="project",
    )(x, cot, gain, ids, w_qkv, w_qkv, w_qkv, w_out)


def attend_kernel(recv_ref, send_ref, kx, vx, kvt, idm, sc, acc):
    lane = lanes((TOK, TOK))
    feature = lane.astype(F32) - HEAD_DIM

    def prepare(c, largest):
        kv = recv_ref[c, :TOK, :].astype(F32)
        idrow = recv_ref[c, OUT_ROWS:, :].astype(F32)[:1]
        idm[pl.ds(c, 1), :] = idrow
        idcol = jnp.broadcast_to(idrow, (TOK, TOK)).T
        extra = jnp.where((feature == idcol) | ((feature > HEADS) & (feature < HEADS + 4)), 1.0, 0.0)
        rows = pl.ds(pl.multiple_of(c * TOK, TOK), TOK)
        kx[rows, :] = jnp.where(lane < HEAD_DIM, kv, extra).astype(BF16)
        vx[rows, :] = jnp.where(lane < HEAD_DIM, jnp.where(lane < 3, 1.0, 0.0), kv).astype(BF16)
        flipped = kv.T
        kvt[:TOK, rows] = flipped.astype(BF16)
        kvt[TOK:, rows] = jnp.ones((16, TOK), BF16)
        acc[rows, :] = jnp.zeros((TOK, TOK), F32)
        norm = jnp.sum(flipped[:HEAD_DIM] * flipped[:HEAD_DIM], axis=0, keepdims=True)
        return jnp.maximum(largest, norm)

    largest = lax.fori_loop(0, N_CTX, prepare, jnp.zeros((1, TOK), F32), unroll=4)
    key_norm = jnp.max(largest)
    for c in range(N_CTX, (SEQ + TK) // TOK):
        rows = slice(c * TOK, (c + 1) * TOK)
        kx[rows, :] = jnp.where(feature == HEADS, 1.0, 0.0).astype(BF16)
        vx[rows, :] = jnp.zeros((TOK, TOK), BF16)
        kvt[:, rows] = jnp.zeros((TOK + 16, TOK), BF16)

    lane_q = lanes((TQ, TOK))
    feature_q = lane_q.astype(F32) - HEAD_DIM
    row_t = lax.broadcasted_iota(jnp.int32, (TOK, TQ), 0)

    def three(row, start, rest):
        hi = row.astype(BF16).astype(F32)
        mid = (row - hi).astype(BF16).astype(F32)
        low = row - hi - mid
        for n, part in enumerate((hi, mid, low)):
            rest = jnp.where(row_t == start + n, part, rest)
        return rest.astype(BF16)

    def query_block(i, carry):
        c0 = i * Q_SRC
        qd = recv_ref[pl.ds(c0, Q_SRC), TOK:OUT_ROWS, :].reshape(TQ, TOK).astype(F32)
        idcols = []
        lowest, highest = None, None
        for a in range(Q_SRC):
            both = recv_ref[c0 + a, OUT_ROWS:, :].astype(F32)
            idcols.append(jnp.broadcast_to(both[8:9], (TOK, TOK)).T[:HALF])
            lowest = both if lowest is None else jnp.minimum(lowest, both)
            highest = both if highest is None else jnp.maximum(highest, both)
        idcol = jnp.concatenate(idcols, axis=0)
        every = idm[...]
        below = jnp.sum(jnp.where(every < jnp.min(lowest), 1.0, 0.0)).astype(jnp.int32)
        upto = jnp.sum(jnp.where(every <= jnp.max(highest), 1.0, 0.0)).astype(jnp.int32)
        start = below // TOK
        steps = (upto - start * TOK + (TK - 1)) // TK

        qdt = qd.T
        other = jnp.where((feature_q != idcol) & (feature_q < HEADS + 1), MASK, 0.0)
        qxt_f = jnp.where(lane_q < HEAD_DIM, qd * 0.125, other).T
        norms = jnp.sum(qxt_f[:HEAD_DIM] * qxt_f[:HEAD_DIM], axis=0, keepdims=True)
        small = jnp.max(norms) * key_norm < 1600.0

        def at(kb, t, size):
            return pl.ds(pl.multiple_of(start * TOK + kb * TK + t * size, TOK), size)

        def largest_step(kb, top):
            for t in range(TK // SUB):
                s = dot_nn(kx[at(kb, t, SUB), :], qxt_f.astype(BF16))
                for r in range(0, SUB, 8):
                    top = jnp.maximum(top, s[r:r + 8])
            return top

        top = lax.fori_loop(0, jnp.where(small, 0, steps), largest_step, jnp.full((8, TQ), MASK, F32))
        top = jnp.where(small, 0.0, jnp.max(top, axis=0, keepdims=True))
        qxt = three(-top, HEAD_DIM + HEADS + 1, qxt_f)

        def value_step(kb, ot):
            tiles = [at(kb, t, SUB) for t in range(TK // SUB)]
            e = [jnp.exp(dot_nn(kx[rows, :], qxt)).astype(BF16) for rows in tiles]
            for rows, part in zip(tiles, e):
                ot = ot + dot_nn(kvt[HEAD_DIM:, rows], part)
            for rows, part in zip(tiles, e):
                sc[rows, :] = part
            return ot

        ot = lax.fori_loop(0, steps, value_step, jnp.zeros((HEAD_DIM + 16, TQ), F32))
        inv = 1.0 / ot[HEAD_DIM:HEAD_DIM + 1]
        ot = (ot[:HEAD_DIM] * inv).astype(BF16).astype(F32)
        delta = jnp.sum(ot * qdt[HEAD_DIM:], axis=0, keepdims=True)
        gxt = three(-delta, 0, jnp.where(row_t < HEAD_DIM, 0.0, qdt))

        scaled = (qdt * inv).T
        right = jnp.concatenate(
            [
                jnp.where(lane_q < HEAD_DIM, scaled * 0.125, 0.0).astype(BF16),
                jnp.where(lane_q >= HEAD_DIM, scaled, 0.0).astype(BF16),
            ],
            axis=0,
        )

        def grad_step(kb, dqt):
            tiles = [at(kb, t, SUB) for t in range(TK // SUB)]
            e = [sc[rows, :] for rows in tiles]
            ds = [part * dot_nn(vx[rows, :], gxt).astype(BF16) for rows, part in zip(tiles, e)]
            for rows, part in zip(tiles, ds):
                dqt = dqt + dot_nn(kvt[:HEAD_DIM, rows], part)
            added = [
                acc[rows, :] + dot_nn(jnp.concatenate([a, b], axis=1), right)
                for rows, a, b in zip(tiles, ds, e)
            ]
            for rows, part in zip(tiles, added):
                acc[rows, :] = part
            return dqt

        dqt = lax.fori_loop(0, steps, grad_step, jnp.zeros((HEAD_DIM, TQ), F32))
        both = jnp.concatenate([ot, dqt * (inv * 0.125)], axis=0).T.astype(BF16)
        for a in range(Q_SRC):
            send_ref[(c0 + a) % N_R, (c0 + a) // N_R, TOK:, :] = both[a * HALF:(a + 1) * HALF]
        return carry

    lax.fori_loop(0, N_QB, query_block, 0)

    def finish(c, carry):
        rows = pl.ds(pl.multiple_of(c * TOK, TOK), TOK)
        send_ref[c % N_R, c // N_R, :TOK, :] = acc[rows, :].astype(BF16)
        return carry

    lax.fori_loop(0, N_CTX, finish, 0, unroll=4)


def attend(recv):
    vmem = pl.BlockSpec(memory_space=pltpu.VMEM)
    padded = SEQ + TK
    return pl.pallas_call(
        attend_kernel,
        in_specs=[vmem],
        out_specs=vmem,
        out_shape=jax.ShapeDtypeStruct((N_R, N_X, OUT_ROWS, TOK), BF16),
        scratch_shapes=[
            pltpu.VMEM((padded, TOK), BF16),
            pltpu.VMEM((padded, TOK), BF16),
            pltpu.VMEM((TOK + 16, padded), BF16),
            pltpu.VMEM((N_CTX, TOK), F32),
            pltpu.VMEM((padded, TQ), BF16),
            pltpu.VMEM((padded, TOK), F32),
        ],
        compiler_params=pltpu.CompilerParams(vmem_limit_bytes=VMEM),
        cost_estimate=pl.CostEstimate(flops=25 * 10**9, bytes_accessed=4 * 10**6, transcendentals=0),
        name="attend",
    )(recv)


def unproject_kernel(me_ref, a_ref, b_ref, c_ref, d_ref, x_ref, gain_ref, wqkv_ref, wo_ref, out_ref, gx_ref):
    result = jnp.zeros((TOK, D), F32)
    g = jnp.zeros((TOK, D), F32)
    for d, ref in enumerate((a_ref, b_ref, c_ref, d_ref)):
        start = (me_ref[0] ^ d) * 256
        result = result + dot_nn(ref[:, 768:], wo_ref[pl.ds(pl.multiple_of(start, 256), 256), :])
        for n in range(3):
            cols = pl.ds(pl.multiple_of(start + n * D, 256), 256)
            g = g + dot_nt(ref[:, n * 256:(n + 1) * 256], wqkv_ref[:, cols])
    out_ref[...] = result.astype(BF16)
    x = x_ref[...].astype(F32)
    cen = x - jnp.mean(x, axis=1, keepdims=True)
    inv = lax.rsqrt(jnp.mean(cen * cen, axis=1, keepdims=True) + EPSILON)
    x_hat = cen * inv
    g = g * gain_ref[...]
    gx = inv * (
        g - jnp.mean(g, axis=1, keepdims=True) - x_hat * jnp.mean(g * x_hat, axis=1, keepdims=True)
    )
    gx_ref[...] = gx.astype(BF16)


def unproject(me, pieces, x, gain, w_qkv, w_out):
    vmem = pl.BlockSpec(memory_space=pltpu.VMEM)
    return pl.pallas_call(
        unproject_kernel,
        in_specs=[pl.BlockSpec(memory_space=pltpu.SMEM)] + [vmem] * 8,
        out_specs=[vmem] * 2,
        out_shape=[jax.ShapeDtypeStruct((TOK, D), BF16)] * 2,
        compiler_params=pltpu.CompilerParams(vmem_limit_bytes=VMEM),
        cost_estimate=pl.CostEstimate(flops=7 * 10**9, bytes_accessed=10**7, transcendentals=0),
        name="unproject",
    )(me, *pieces, x, gain, w_qkv, w_out)


def weights_kernel(me_ref, recv_ref, b0, b1, b2, b3, cols_ref, send_ref):
    for i in range(N_X):
        at = me_ref[0] ^ i
        parts = [[], [], [], []]
        for h in range(4):
            lo, hi = recv_ref[2 * h, at].astype(F32), recv_ref[2 * h + 1, at].astype(F32)
            kv = lo[:TOK] + hi[:TOK]
            aq = jnp.concatenate([lo[TOK:], hi[TOK:]], axis=0)
            parts[0].append(aq[:, HEAD_DIM:])
            parts[1].append(kv[:, :HEAD_DIM])
            parts[2].append(kv[:, HEAD_DIM:])
            parts[3].append(aq[:, :HEAD_DIM])
        for n, part in enumerate(parts):
            cols_ref[i, :, n * 256:(n + 1) * 256] = jnp.concatenate(part, axis=1).astype(BF16)
    cols = cols_ref[...].reshape(N_X * TOK, D)
    both = jnp.concatenate([b0[...], b1[...], b2[...], b3[...]], axis=0)
    for m in range(4):
        part = dot_tn(both[:, m * 256:(m + 1) * 256], cols[:, :768])
        for r in range(N_R):
            send_ref[8 * m + r, :, :768] = part[32 * r:32 * r + 32].astype(BF16)
    for m in range(N_GRP):
        part = dot_tn(cols[:, 768:], both[:, D + m * 256:D + (m + 1) * 256])
        for r in range(N_R):
            send_ref[8 * m + r, :, 768:] = part[32 * r:32 * r + 32].astype(BF16)


def weights(me, recv, both):
    vmem = pl.BlockSpec(memory_space=pltpu.VMEM)
    return pl.pallas_call(
        weights_kernel,
        in_specs=[pl.BlockSpec(memory_space=pltpu.SMEM)] + [vmem] * 5,
        out_specs=[vmem] * 2,
        out_shape=[
            jax.ShapeDtypeStruct((N_X, TOK, D), BF16),
            jax.ShapeDtypeStruct((N_CTX, 32, D), BF16),
        ],
        compiler_params=pltpu.CompilerParams(vmem_limit_bytes=VMEM),
        name="weights",
    )(me, recv, *both)


def assemble_kernel(me_ref, a_ref, b_ref, c_ref, d_ref, qkv_ref, out_ref):
    for d, ref in enumerate((a_ref, b_ref, c_ref, d_ref)):
        start = (me_ref[0] ^ d) * 256
        part = ref[...].astype(F32)
        for n in range(3):
            cols = pl.ds(pl.multiple_of(start + n * D, 256), 256)
            qkv_ref[:, cols] = part[:, n * 256:(n + 1) * 256]
        out_ref[:, pl.ds(pl.multiple_of(start, 256), 256)] = part[:, 768:]


def assemble(me, parts):
    vmem = pl.BlockSpec(memory_space=pltpu.VMEM)
    return pl.pallas_call(
        assemble_kernel,
        in_specs=[pl.BlockSpec(memory_space=pltpu.SMEM)] + [vmem] * 4,
        out_specs=[vmem] * 2,
        out_shape=[jax.ShapeDtypeStruct((32, 3 * D), F32), jax.ShapeDtypeStruct((32, D), F32)],
        name="assemble",
    )(me, *parts)


def swap(piece, axis, d):
    return piece if d == 0 else lax.ppermute(piece, axis, [(i, i ^ d) for i in range(4)])


def shards(patches, gain, w_qkv, w_out, image_ids, grad_out):
    x, cot = patches[0], grad_out[0]
    gain_row = gain[None]
    me = lax.axis_index("x").astype(jnp.int32)[None]
    send, both = project(x, cot, gain_row, image_ids, w_qkv, w_out)
    recv = lax.all_to_all(send, ("x", "r"), 0, 0, tiled=True)
    recv, both = lax.optimization_barrier((recv, both))
    both = [swap(both, "x", d) for d in range(N_X)]
    done, both = lax.optimization_barrier((attend(recv), both))
    back = lax.all_to_all(done, "r", 0, 0, tiled=True)
    cols, terms = weights(me, back, both)
    cols = [swap(cols[d], "x", d) for d in range(N_X)]
    parts = lax.all_to_all(terms, ("grp", "r"), 0, 0, tiled=True)
    out, grad_x = unproject(me, cols, x, gain_row, w_qkv, w_out)
    parts, out, grad_x = lax.optimization_barrier((parts, out, grad_x))
    factor = 1.0 / math.sqrt(N_GRP * SEQ)
    share = (jnp.sum(parts.astype(F32), axis=0) * factor).astype(BF16)
    flip = [(s * N_X + j, j * N_X + s) for s in range(N_GRP) for j in range(N_X)]
    share_qkv = lax.ppermute(share[:, :768], ("grp", "x"), flip)
    share = jnp.concatenate([share_qkv, share[:, 768:]], axis=1)
    shares = [swap(share, "grp", d) for d in range(N_GRP)]
    grad_qkv, grad_w_out = assemble(lax.axis_index("grp").astype(jnp.int32)[None], shares)
    return out[None], grad_x[None], grad_qkv, grad_w_out


def solution(mesh):
    fine = Mesh(mesh.devices.reshape(N_GRP, N_X, N_R), ("grp", "x", "r"))
    ctx = ("x", "r")
    in_specs = (P("grp", ctx, None), P(), P(), P(), P("grp", ctx), P("grp", ctx, None))
    out_specs = (P("grp", ctx, None), P("grp", ctx, None), P(ctx, None), P(ctx, None))
    return jax.shard_map(shards, mesh=fine, in_specs=in_specs, out_specs=out_specs, check_vma=False)
```

```python
import functools
import math

import jax
import jax.numpy as jnp
from jax import lax
from jax.experimental import pallas as pl
from jax.experimental.pallas import tpu as pltpu
from jax.sharding import Mesh, PartitionSpec as P

HEADS = 16
HEAD_DIM = 64
D = HEADS * HEAD_DIM
TOK = 128
HALF = TOK // 2
N_CTX = 32
N_GRP = 4
N_X = 4
N_R = 8
SEQ = TOK * N_CTX
ID_ROWS = 16
IN_ROWS = TOK + HALF + ID_ROWS
OUT_ROWS = TOK + HALF
TQ = 256
LARGE, MIDDLE, SMALL = 2176, 896, 384
SUB = 128
Q_SRC = TQ // HALF
N_QB = N_CTX // Q_SRC
EPSILON = 1e-06
MASK = -1e30
MIB = 1024 * 1024
F32 = jnp.float32
BF16 = jnp.bfloat16


def dot_nn(a, b):
    return jnp.dot(a, b, preferred_element_type=F32)


def dot_nt(a, b):
    return lax.dot_general(a, b, (((1,), (1,)), ((), ())), preferred_element_type=F32)


def dot_tn(a, b):
    return lax.dot_general(a, b, (((0,), (0,)), ((), ())), preferred_element_type=F32)


def lanes(shape):
    return lax.broadcasted_iota(jnp.int32, shape, 1)


def fetch(wqkv_hbm, wo_hbm, wqkv, wo, sems, n, start):
    start = start if isinstance(start, int) else pl.multiple_of(start, 256)
    copies = [pltpu.make_async_copy(wo_hbm.at[pl.ds(start, 256), :], wo.at[n], sems.at[n, 3])]
    for m in range(3):
        cols = pl.ds(start + m * D, 256)
        copies.append(pltpu.make_async_copy(wqkv_hbm.at[:, cols], wqkv.at[n, m], sems.at[n, m]))
    return copies


FETCHED = [
    pltpu.VMEM((4, 3, D, 256), BF16),
    pltpu.VMEM((4, 256, D), BF16),
    pltpu.SemaphoreType.DMA((4, 4)),
]


def project_kernel(x_hbm, cot_hbm, gain_hbm, ids_hbm, wqkv_hbm, wo_hbm, send_ref, both_ref, x_ref, gain_ref, ids_ref, wqkv, wo, sems, in_sems):
    cot_ref = both_ref.at[:, D:]
    arrays = ((x_hbm, x_ref), (gain_hbm, gain_ref), (ids_hbm, ids_ref), (cot_hbm, cot_ref))
    inputs = [pltpu.make_async_copy(*pair, in_sems.at[n]) for n, pair in enumerate(arrays)]
    copies = [fetch(wqkv_hbm, wo_hbm, wqkv, wo, sems, n, n * 256) for n in range(4)]
    for copy in inputs + copies[0]:
        copy.start()
    for copy in inputs[:3]:
        copy.wait()
    for group in copies[1:]:
        for copy in group:
            copy.start()
    x = x_ref[...].astype(F32)
    cen = x - jnp.mean(x, axis=1, keepdims=True)
    inv = lax.rsqrt(jnp.mean(cen * cen, axis=1, keepdims=True) + EPSILON)
    n = (cen * inv * gain_ref[...]).astype(BF16)
    both_ref[:, :D] = n
    ids = ids_ref[...].astype(F32)
    rolled = jnp.concatenate([ids[:, HALF:], ids[:, :HALF]], axis=1)
    inputs[3].wait()
    for j in range(4):
        for copy in copies[j]:
            copy.wait()
        g = dot_nt(cot_ref[...], wo[j])
        q, k, v = (dot_nn(n, wqkv[j, m]) for m in range(3))
        for h in range(4):
            cols = slice(h * HEAD_DIM, (h + 1) * HEAD_DIM)
            kv = jnp.concatenate([k[:, cols], v[:, cols]], axis=1).astype(BF16)
            qg = jnp.concatenate([q[:, cols], g[:, cols]], axis=1).astype(BF16)
            for p in range(2):
                own = ids if p == 0 else rolled
                rows = jnp.concatenate(
                    [jnp.broadcast_to(ids, (8, TOK)), jnp.broadcast_to(own, (8, TOK))], axis=0
                )
                to = 8 * j + 2 * h + p
                send_ref[to, :TOK, :] = kv
                send_ref[to, TOK:OUT_ROWS, :] = qg[p * HALF:(p + 1) * HALF, :]
                send_ref[to, OUT_ROWS:, :] = rows.astype(BF16)


def project(x, cot, gain, ids, w_qkv, w_out):
    vmem = pl.BlockSpec(memory_space=pltpu.VMEM)
    hbm = pl.BlockSpec(memory_space=pltpu.HBM)
    return pl.pallas_call(
        project_kernel,
        in_specs=[hbm] * 6,
        out_specs=[vmem] * 2,
        out_shape=[
            jax.ShapeDtypeStruct((N_CTX, IN_ROWS, TOK), BF16),
            jax.ShapeDtypeStruct((TOK, 2 * D), BF16),
        ],
        scratch_shapes=[
            pltpu.VMEM((TOK, D), BF16),
            pltpu.VMEM((1, D), F32),
            pltpu.VMEM((1, TOK), jnp.int32),
            *FETCHED,
            pltpu.SemaphoreType.DMA((4,)),
        ],
        compiler_params=pltpu.CompilerParams(vmem_limit_bytes=56 * MIB),
        name="project",
    )(x, cot, gain, ids, w_qkv, w_out)


def attend_kernel(recv_ref, send_ref, kx, vx, kvt, idm, sc, acc):
    lane = lanes((TOK, TOK))
    feature = lane.astype(F32) - HEAD_DIM

    def prepare(c, largest):
        kv = recv_ref[c, :TOK, :].astype(F32)
        idrow = recv_ref[c, OUT_ROWS:, :].astype(F32)[:1]
        idm[pl.ds(c, 1), :] = idrow
        idcol = jnp.broadcast_to(idrow, (TOK, TOK)).T
        extra = jnp.where((feature == idcol) | ((feature > HEADS) & (feature < HEADS + 4)), 1.0, 0.0)
        rows = pl.ds(pl.multiple_of(c * TOK, TOK), TOK)
        kx[rows, :] = jnp.where(lane < HEAD_DIM, kv, extra).astype(BF16)
        vx[rows, :] = jnp.where(lane < HEAD_DIM, jnp.where(lane < 3, 1.0, 0.0), kv).astype(BF16)
        flipped = kv.T
        kvt[:TOK, rows] = flipped.astype(BF16)
        kvt[TOK:, rows] = jnp.ones((16, TOK), BF16)
        acc[rows, :] = jnp.zeros((TOK, TOK), F32)
        norm = jnp.sum(flipped[:HEAD_DIM] * flipped[:HEAD_DIM], axis=0, keepdims=True)
        return jnp.maximum(largest, norm)

    largest = lax.fori_loop(0, N_CTX, prepare, jnp.zeros((1, TOK), F32), unroll=4)
    key_norm = jnp.max(largest)
    for c in range(N_CTX, (SEQ + LARGE) // TOK):
        rows = slice(c * TOK, (c + 1) * TOK)
        kx[rows, :] = jnp.where(feature == HEADS, 1.0, 0.0).astype(BF16)
        vx[rows, :] = jnp.zeros((TOK, TOK), BF16)
        kvt[:, rows] = jnp.zeros((TOK + 16, TOK), BF16)

    lane_q = lanes((TQ, TOK))
    feature_q = lane_q.astype(F32) - HEAD_DIM
    row_t = lax.broadcasted_iota(jnp.int32, (TOK, TQ), 0)

    def three(row, start, rest):
        hi = row.astype(BF16).astype(F32)
        mid = (row - hi).astype(BF16).astype(F32)
        low = row - hi - mid
        for n, part in enumerate((hi, mid, low)):
            rest = jnp.where(row_t == start + n, part, rest)
        return rest.astype(BF16)

    def query_block(i, carry):
        c0 = i * Q_SRC
        qd = recv_ref[pl.ds(c0, Q_SRC), TOK:OUT_ROWS, :].reshape(TQ, TOK).astype(F32)
        idcols = []
        lowest, highest = None, None
        for a in range(Q_SRC):
            both = recv_ref[c0 + a, OUT_ROWS:, :].astype(F32)
            idcols.append(jnp.broadcast_to(both[8:9], (TOK, TOK)).T[:HALF])
            lowest = both if lowest is None else jnp.minimum(lowest, both)
            highest = both if highest is None else jnp.maximum(highest, both)
        idcol = jnp.concatenate(idcols, axis=0)
        every = idm[...]
        below = jnp.sum(jnp.where(every < jnp.min(lowest), 1.0, 0.0)).astype(jnp.int32)
        upto = jnp.sum(jnp.where(every <= jnp.max(highest), 1.0, 0.0)).astype(jnp.int32)
        start = below // TOK
        extent = upto - start * TOK
        n_large = (extent + (LARGE - 1 - MIDDLE - SMALL)) // LARGE
        extent = jnp.maximum(extent - n_large * LARGE, 0)
        n_middle = (extent + (MIDDLE - 1 - SMALL)) // MIDDLE
        n_small = (jnp.maximum(extent - n_middle * MIDDLE, 0) + (SMALL - 1)) // SMALL

        qdt = qd.T
        other = jnp.where((feature_q != idcol) & (feature_q < HEADS + 1), MASK, 0.0)
        qxt_f = jnp.where(lane_q < HEAD_DIM, qd * 0.125, other).T
        norms = jnp.sum(qxt_f[:HEAD_DIM] * qxt_f[:HEAD_DIM], axis=0, keepdims=True)
        small = jnp.max(norms) * key_norm < 1600.0

        def steps(step, state, wanted=True):
            def run(first, size):
                def body(n, state):
                    base = first + n * size
                    return step(
                        [
                            pl.ds(pl.multiple_of(base + t * SUB, TOK), SUB)
                            for t in range(size // SUB)
                        ],
                        state,
                    )

                return body

            first = start * TOK
            for size, count in ((LARGE, n_large), (MIDDLE, n_middle), (SMALL, n_small)):
                state = lax.fori_loop(0, jnp.where(wanted, count, 0), run(first, size), state)
                first = first + count * size
            return state

        def largest_step(tiles, top):
            for rows in tiles:
                s = dot_nn(kx[rows, :], qxt_f.astype(BF16))
                for r in range(0, SUB, 8):
                    top = jnp.maximum(top, s[r:r + 8])
            return top

        top = steps(largest_step, jnp.full((8, TQ), MASK, F32), ~small)
        top = jnp.where(small, 0.0, jnp.max(top, axis=0, keepdims=True))
        qxt = three(-top, HEAD_DIM + HEADS + 1, qxt_f)

        def value_step(tiles, ot):
            e = [jnp.exp(dot_nn(kx[rows, :], qxt)).astype(BF16) for rows in tiles]
            for n in range(0, len(tiles), 2):
                k = min(2, len(tiles) - n)
                rows = pl.ds(pl.multiple_of(tiles[n].start, TOK), k * SUB)
                ot = ot + dot_nn(kvt[HEAD_DIM:, rows], jnp.concatenate(e[n:n + k], axis=0))
            for rows, part in zip(tiles, e):
                sc[rows, :] = part
            return ot

        ot = steps(value_step, jnp.zeros((HEAD_DIM + 16, TQ), F32))
        inv = 1.0 / ot[HEAD_DIM:HEAD_DIM + 1]
        ot = (ot[:HEAD_DIM] * inv).astype(BF16).astype(F32)
        delta = jnp.sum(ot * qdt[HEAD_DIM:], axis=0, keepdims=True)
        gxt = three(-delta, 0, jnp.where(row_t < HEAD_DIM, 0.0, qdt))

        scaled = (qdt * inv).T
        right = jnp.concatenate(
            [
                jnp.where(lane_q < HEAD_DIM, scaled * 0.125, 0.0).astype(BF16),
                jnp.where(lane_q >= HEAD_DIM, scaled, 0.0).astype(BF16),
            ],
            axis=0,
        )

        def grad_step(tiles, dqt):
            e = [sc[rows, :] for rows in tiles]
            ds = [part * dot_nn(vx[rows, :], gxt).astype(BF16) for rows, part in zip(tiles, e)]
            for n in range(0, len(tiles), 2):
                k = min(2, len(tiles) - n)
                rows = pl.ds(pl.multiple_of(tiles[n].start, TOK), k * SUB)
                dqt = dqt + dot_nn(kvt[:HEAD_DIM, rows], jnp.concatenate(ds[n:n + k], axis=0))
            added = [
                acc[rows, :] + dot_nn(jnp.concatenate([a, b], axis=1), right)
                for rows, a, b in zip(tiles, ds, e)
            ]
            for rows, part in zip(tiles, added):
                acc[rows, :] = part
            return dqt

        dqt = steps(grad_step, jnp.zeros((HEAD_DIM, TQ), F32))
        both = jnp.concatenate([ot, dqt * (inv * 0.125)], axis=0).T.astype(BF16)
        for a in range(Q_SRC):
            send_ref[(c0 + a) % N_R, (c0 + a) // N_R, TOK:, :] = both[a * HALF:(a + 1) * HALF]
        return carry

    lax.fori_loop(0, N_QB, query_block, 0)

    def finish(c, carry):
        rows = pl.ds(pl.multiple_of(c * TOK, TOK), TOK)
        send_ref[c % N_R, c // N_R, :TOK, :] = acc[rows, :].astype(BF16)
        return carry

    lax.fori_loop(0, N_CTX, finish, 0, unroll=4)


def attend(recv):
    vmem = pl.BlockSpec(memory_space=pltpu.VMEM)
    padded = SEQ + LARGE
    return pl.pallas_call(
        attend_kernel,
        in_specs=[vmem],
        out_specs=vmem,
        out_shape=jax.ShapeDtypeStruct((N_R, N_X, OUT_ROWS, TOK), BF16),
        scratch_shapes=[
            pltpu.VMEM((padded, TOK), BF16),
            pltpu.VMEM((padded, TOK), BF16),
            pltpu.VMEM((TOK + 16, padded), BF16),
            pltpu.VMEM((N_CTX, TOK), F32),
            pltpu.VMEM((padded, TQ), BF16),
            pltpu.VMEM((padded, TOK), F32),
        ],
        compiler_params=pltpu.CompilerParams(vmem_limit_bytes=28 * MIB),
        cost_estimate=pl.CostEstimate(flops=25 * 10**9, bytes_accessed=4 * 10**6, transcendentals=0),
        name="attend",
    )(recv)


def unproject_kernel(me_ref, c0, c1, c2, c3, x_hbm, gain_hbm, wqkv_hbm, wo_hbm, out_ref, gx_ref, x_ref, gain_ref, wqkv, wo, sems, in_sems):
    copies = [
        fetch(wqkv_hbm, wo_hbm, wqkv, wo, sems, d, (me_ref[0] ^ d) * 256) for d in range(N_X)
    ]
    for group in copies:
        for copy in group:
            copy.start()
    inputs = [
        pltpu.make_async_copy(x_hbm, x_ref, in_sems.at[0]),
        pltpu.make_async_copy(gain_hbm, gain_ref, in_sems.at[1]),
    ]
    for copy in inputs:
        copy.start()
    result = jnp.zeros((TOK, D), F32)
    g = jnp.zeros((TOK, D), F32)
    for d, ref in enumerate((c0, c1, c2, c3)):
        for copy in copies[d]:
            copy.wait()
        result = result + dot_nn(ref[:, 768:], wo[d])
        for m in range(3):
            g = g + dot_nt(ref[:, m * 256:(m + 1) * 256], wqkv[d, m])
    out_ref[...] = result.astype(BF16)
    for copy in inputs:
        copy.wait()
    x = x_ref[...].astype(F32)
    cen = x - jnp.mean(x, axis=1, keepdims=True)
    inv = lax.rsqrt(jnp.mean(cen * cen, axis=1, keepdims=True) + EPSILON)
    x_hat = cen * inv
    g = g * gain_ref[...]
    gx = inv * (
        g - jnp.mean(g, axis=1, keepdims=True) - x_hat * jnp.mean(g * x_hat, axis=1, keepdims=True)
    )
    gx_ref[...] = gx.astype(BF16)


def unproject(me, pieces, x, gain, w_qkv, w_out):
    vmem = pl.BlockSpec(memory_space=pltpu.VMEM)
    hbm = pl.BlockSpec(memory_space=pltpu.HBM)
    return pl.pallas_call(
        unproject_kernel,
        in_specs=[pl.BlockSpec(memory_space=pltpu.SMEM)] + [vmem] * 4 + [hbm] * 4,
        out_specs=[vmem] * 2,
        out_shape=[jax.ShapeDtypeStruct((TOK, D), BF16)] * 2,
        scratch_shapes=[
            pltpu.VMEM((TOK, D), BF16),
            pltpu.VMEM((1, D), F32),
            *FETCHED,
            pltpu.SemaphoreType.DMA((2,)),
        ],
        compiler_params=pltpu.CompilerParams(vmem_limit_bytes=56 * MIB),
        cost_estimate=pl.CostEstimate(flops=7 * 10**9, bytes_accessed=10**7, transcendentals=0),
        name="unproject",
    )(me, *pieces, x, gain, w_qkv, w_out)


def repack_kernel(me_ref, recv_ref, *cols_refs):
    for d, cols_ref in enumerate(cols_refs):
        at = me_ref[0] ^ d
        parts = [[], [], [], []]
        for h in range(4):
            lo, hi = recv_ref[2 * h, at].astype(F32), recv_ref[2 * h + 1, at].astype(F32)
            kv = lo[:TOK] + hi[:TOK]
            aq = jnp.concatenate([lo[TOK:], hi[TOK:]], axis=0)
            parts[0].append(aq[:, HEAD_DIM:])
            parts[1].append(kv[:, :HEAD_DIM])
            parts[2].append(kv[:, HEAD_DIM:])
            parts[3].append(aq[:, :HEAD_DIM])
        for n, part in enumerate(parts):
            cols_ref[:, n * 256:(n + 1) * 256] = jnp.concatenate(part, axis=1).astype(BF16)


def repack(me, recv):
    vmem = pl.BlockSpec(memory_space=pltpu.VMEM)
    return pl.pallas_call(
        repack_kernel,
        in_specs=[pl.BlockSpec(memory_space=pltpu.SMEM), vmem],
        out_specs=[vmem] * N_X,
        out_shape=[jax.ShapeDtypeStruct((TOK, D), BF16)] * N_X,
        compiler_params=pltpu.CompilerParams(vmem_limit_bytes=16 * MIB),
        name="repack",
    )(me, recv)


def weights_kernel(me_ref, c0, c1, c2, c3, b0, b1, b2, b3, own_ref, other_ref):
    cols_refs = (c0, c1, c2, c3)
    cols = jnp.concatenate([ref[...] for ref in cols_refs], axis=0)
    both = jnp.concatenate([b0[...], b1[...], b2[...], b3[...]], axis=0)
    first_core = me_ref[1] == 0
    for zl in range(2):
        parts = []
        for m in (2 * zl, 2 * zl + 1):
            left = dot_tn(both[:, m * 256:(m + 1) * 256], cols[:, :768])
            right = dot_tn(cols[:, 768:], both[:, D + m * 256:D + (m + 1) * 256])
            parts.append((left, right))
        for n in range(2):
            cols_of = slice(0, 768) if n == 0 else slice(768, D)
            own = jnp.where(first_core, parts[0][n], parts[1][n]).astype(BF16)
            other = jnp.where(first_core, parts[1][n], parts[0][n]).astype(BF16)
            for r in range(N_R):
                own_ref[8 * zl + r, :, cols_of] = own[32 * r:32 * r + 32]
                other_ref[8 * zl + r, :, cols_of] = other[32 * r:32 * r + 32]


def weights(me, cols, both):
    vmem = pl.BlockSpec(memory_space=pltpu.VMEM)
    return pl.pallas_call(
        weights_kernel,
        in_specs=[pl.BlockSpec(memory_space=pltpu.SMEM)] + [vmem] * 8,
        out_specs=[vmem] * 2,
        out_shape=[jax.ShapeDtypeStruct((N_CTX // 2, 32, D), BF16)] * 2,
        cost_estimate=pl.CostEstimate(flops=2 * 10**9, bytes_accessed=4 * 10**6, transcendentals=0),
        compiler_params=pltpu.CompilerParams(vmem_limit_bytes=24 * MIB),
        name="weights",
    )(me, *cols, *both)


def assemble_kernel(me_ref, a_ref, b_ref, c_ref, d_ref, qkv_ref, out_ref):
    for d, ref in enumerate((a_ref, b_ref, c_ref, d_ref)):
        start = (me_ref[0] ^ d) * 256
        part = ref[...].astype(F32)
        for n in range(3):
            cols = pl.ds(pl.multiple_of(start + n * D, 256), 256)
            qkv_ref[:, cols] = part[:, n * 256:(n + 1) * 256]
        out_ref[:, pl.ds(pl.multiple_of(start, 256), 256)] = part[:, 768:]


def assemble(me, parts):
    vmem = pl.BlockSpec(memory_space=pltpu.VMEM)
    return pl.pallas_call(
        assemble_kernel,
        in_specs=[pl.BlockSpec(memory_space=pltpu.SMEM)] + [vmem] * 4,
        out_specs=[vmem] * 2,
        out_shape=[jax.ShapeDtypeStruct((32, 3 * D), F32), jax.ShapeDtypeStruct((32, D), F32)],
        compiler_params=pltpu.CompilerParams(vmem_limit_bytes=8 * MIB),
        name="assemble",
    )(me, *parts)


def swap(piece, axis, d):
    return piece if d == 0 else lax.ppermute(piece, axis, [(i, i ^ d) for i in range(4)])


def shards(patches, gain, w_qkv, w_out, image_ids, grad_out):
    x, cot = patches[0], grad_out[0]
    gain_row = gain[None]
    me = jnp.stack([lax.axis_index("x"), lax.axis_index("core")]).astype(jnp.int32)
    send, both = project(x, cot, gain_row, image_ids, w_qkv, w_out)
    recv = lax.all_to_all(send, ("x", "r"), 0, 0, tiled=True)
    recv, both = lax.optimization_barrier((recv, both))
    both = [swap(both, "x", d) for d in range(N_X)]
    done, both = lax.optimization_barrier((attend(recv), both))
    back = lax.all_to_all(done, "r", 0, 0, tiled=True)
    cols = repack(me, back)
    own, other = weights(me, cols, both)
    got = lax.ppermute(other, "core", [(0, 1), (1, 0)])
    cols = [swap(cols[d], "x", d) for d in range(N_X)]
    terms = (own.astype(F32) + got.astype(F32)).astype(BF16)
    parts = lax.all_to_all(terms, ("zl", "r"), 0, 0, tiled=True)
    out, grad_x = unproject(me, cols, x, gain_row, w_qkv, w_out)
    factor = 1.0 / math.sqrt(N_GRP * SEQ)
    share = (jnp.sum(parts.astype(F32), axis=0) * factor).astype(BF16)
    flip = [(s * N_X + j, j * N_X + s) for s in range(N_GRP) for j in range(N_X)]
    share_qkv = lax.ppermute(share[:, :768], ("zl", "core", "x"), flip)
    share = jnp.concatenate([share_qkv, share[:, 768:]], axis=1)
    shares = [swap(share, ("zl", "core"), d) for d in range(N_GRP)]
    grad_qkv, grad_w_out = assemble(lax.axis_index(("zl", "core")).astype(jnp.int32)[None], shares)
    return out[None], grad_x[None], grad_qkv, grad_w_out


def solution(mesh):
    fine = Mesh(mesh.devices.reshape(2, 2, N_X, N_R), ("zl", "core", "x", "r"))
    grp, ctx = ("zl", "core"), ("x", "r")
    in_specs = (P(grp, ctx, None), P(), P(), P(), P(grp, ctx), P(grp, ctx, None))
    out_specs = (P(grp, ctx, None), P(grp, ctx, None), P(ctx, None), P(ctx, None))
    return jax.shard_map(shards, mesh=fine, in_specs=in_specs, out_specs=out_specs, check_vma=False)
```

```python
import functools
import math

import jax
import jax.numpy as jnp
from jax import lax
from jax.experimental import pallas as pl
from jax.experimental.pallas import tpu as pltpu
from jax.sharding import Mesh, PartitionSpec as P

HEADS = 16
HEAD_DIM = 64
D = HEADS * HEAD_DIM
TOK = 128
HALF = TOK // 2
N_CTX = 32
N_GRP = 4
N_X = 4
N_R = 8
SEQ = TOK * N_CTX
ID_ROWS = 16
IN_ROWS = TOK + HALF + ID_ROWS
OUT_ROWS = TOK + HALF
TQ = 256
LARGE, MIDDLE, SMALL = 2176, 896, 384
SUB = 128
Q_SRC = TQ // HALF
N_QB = N_CTX // Q_SRC
EPSILON = 1e-06
MASK = -1e30
MIB = 1024 * 1024
F32 = jnp.float32
BF16 = jnp.bfloat16


def dot_nn(a, b):
    return jnp.dot(a, b, preferred_element_type=F32)


def dot_nt(a, b):
    return lax.dot_general(a, b, (((1,), (1,)), ((), ())), preferred_element_type=F32)


def dot_tn(a, b):
    return lax.dot_general(a, b, (((0,), (0,)), ((), ())), preferred_element_type=F32)


def lanes(shape):
    return lax.broadcasted_iota(jnp.int32, shape, 1)


def fetch(wqkv_hbm, wo_hbm, wqkv, wo, sems, n, start):
    start = start if isinstance(start, int) else pl.multiple_of(start, 256)
    copies = [pltpu.make_async_copy(wo_hbm.at[pl.ds(start, 256), :], wo.at[n], sems.at[n, 3])]
    for m in range(3):
        cols = pl.ds(start + m * D, 256)
        copies.append(pltpu.make_async_copy(wqkv_hbm.at[:, cols], wqkv.at[n, m], sems.at[n, m]))
    return copies


FETCHED = [
    pltpu.VMEM((4, 3, D, 256), BF16),
    pltpu.VMEM((4, 256, D), BF16),
    pltpu.SemaphoreType.DMA((4, 4)),
]


def project_kernel(x_hbm, cot_hbm, gain_hbm, ids_hbm, wqkv_hbm, wo_hbm, send_ref, both_ref, x_ref, gain_ref, ids_ref, wqkv, wo, sems, in_sems):
    cot_ref = both_ref.at[:, D:]
    arrays = ((x_hbm, x_ref), (gain_hbm, gain_ref), (ids_hbm, ids_ref), (cot_hbm, cot_ref))
    inputs = [pltpu.make_async_copy(*pair, in_sems.at[n]) for n, pair in enumerate(arrays)]
    copies = [fetch(wqkv_hbm, wo_hbm, wqkv, wo, sems, n, n * 256) for n in range(4)]
    for copy in inputs + copies[0]:
        copy.start()
    for copy in inputs[:3]:
        copy.wait()
    for group in copies[1:]:
        for copy in group:
            copy.start()
    x = x_ref[...].astype(F32)
    cen = x - jnp.mean(x, axis=1, keepdims=True)
    inv = lax.rsqrt(jnp.mean(cen * cen, axis=1, keepdims=True) + EPSILON)
    n = (cen * inv * gain_ref[...]).astype(BF16)
    both_ref[:, :D] = n
    ids = ids_ref[...].astype(F32)
    rolled = jnp.concatenate([ids[:, HALF:], ids[:, :HALF]], axis=1)
    inputs[3].wait()
    for j in range(4):
        for copy in copies[j]:
            copy.wait()
        g = dot_nt(cot_ref[...], wo[j])
        q, k, v = (dot_nn(n, wqkv[j, m]) for m in range(3))
        for h in range(4):
            cols = slice(h * HEAD_DIM, (h + 1) * HEAD_DIM)
            kv = jnp.concatenate([k[:, cols], v[:, cols]], axis=1).astype(BF16)
            qg = jnp.concatenate([q[:, cols], g[:, cols]], axis=1).astype(BF16)
            for p in range(2):
                own = ids if p == 0 else rolled
                rows = jnp.concatenate(
                    [jnp.broadcast_to(ids, (8, TOK)), jnp.broadcast_to(own, (8, TOK))], axis=0
                )
                to = 8 * j + 2 * h + p
                send_ref[to, :TOK, :] = kv
                send_ref[to, TOK:OUT_ROWS, :] = qg[p * HALF:(p + 1) * HALF, :]
                send_ref[to, OUT_ROWS:, :] = rows.astype(BF16)


def project(x, cot, gain, ids, w_qkv, w_out):
    vmem = pl.BlockSpec(memory_space=pltpu.VMEM)
    hbm = pl.BlockSpec(memory_space=pltpu.HBM)
    return pl.pallas_call(
        project_kernel,
        in_specs=[hbm] * 6,
        out_specs=[vmem] * 2,
        out_shape=[
            jax.ShapeDtypeStruct((N_CTX, IN_ROWS, TOK), BF16),
            jax.ShapeDtypeStruct((TOK, 2 * D), BF16),
        ],
        scratch_shapes=[
            pltpu.VMEM((TOK, D), BF16),
            pltpu.VMEM((1, D), F32),
            pltpu.VMEM((1, TOK), jnp.int32),
            *FETCHED,
            pltpu.SemaphoreType.DMA((4,)),
        ],
        compiler_params=pltpu.CompilerParams(vmem_limit_bytes=56 * MIB),
        name="project",
    )(x, cot, gain, ids, w_qkv, w_out)


def attend_kernel(recv_ref, send_ref, kx, vx, kvt, idm, sc, acc):
    lane = lanes((TOK, TOK))
    feature = lane.astype(F32) - HEAD_DIM

    def prepare(c, largest):
        kv = recv_ref[c, :TOK, :].astype(F32)
        idrow = recv_ref[c, OUT_ROWS:, :].astype(F32)[:1]
        idm[pl.ds(c, 1), :] = idrow
        idcol = jnp.broadcast_to(idrow, (TOK, TOK)).T
        extra = jnp.where((feature == idcol) | ((feature > HEADS) & (feature < HEADS + 4)), 1.0, 0.0)
        rows = pl.ds(pl.multiple_of(c * TOK, TOK), TOK)
        kx[rows, :] = jnp.where(lane < HEAD_DIM, kv, extra).astype(BF16)
        vx[rows, :] = jnp.where(lane < HEAD_DIM, jnp.where(lane < 3, 1.0, 0.0), kv).astype(BF16)
        flipped = kv.T
        kvt[:TOK, rows] = flipped.astype(BF16)
        kvt[TOK:, rows] = jnp.ones((16, TOK), BF16)
        acc[rows, :] = jnp.zeros((TOK, TOK), F32)
        norm = jnp.sum(flipped[:HEAD_DIM] * flipped[:HEAD_DIM], axis=0, keepdims=True)
        return jnp.maximum(largest, norm)

    largest = lax.fori_loop(0, N_CTX, prepare, jnp.zeros((1, TOK), F32), unroll=4)
    key_norm = jnp.max(largest)
    for c in range(N_CTX, (SEQ + LARGE) // TOK):
        rows = slice(c * TOK, (c + 1) * TOK)
        kx[rows, :] = jnp.where(feature == HEADS, 1.0, 0.0).astype(BF16)
        vx[rows, :] = jnp.zeros((TOK, TOK), BF16)
        kvt[:, rows] = jnp.zeros((TOK + 16, TOK), BF16)

    lane_q = lanes((TQ, TOK))
    feature_q = lane_q.astype(F32) - HEAD_DIM
    row_t = lax.broadcasted_iota(jnp.int32, (TOK, TQ), 0)

    def three(row, start, rest):
        hi = row.astype(BF16).astype(F32)
        mid = (row - hi).astype(BF16).astype(F32)
        low = row - hi - mid
        for n, part in enumerate((hi, mid, low)):
            rest = jnp.where(row_t == start + n, part, rest)
        return rest.astype(BF16)

    def query_block(i, carry):
        c0 = i * Q_SRC
        qd = recv_ref[pl.ds(c0, Q_SRC), TOK:OUT_ROWS, :].reshape(TQ, TOK).astype(F32)
        idcols = []
        lowest, highest = None, None
        for a in range(Q_SRC):
            both = recv_ref[c0 + a, OUT_ROWS:, :].astype(F32)
            idcols.append(jnp.broadcast_to(both[8:9], (TOK, TOK)).T[:HALF])
            lowest = both if lowest is None else jnp.minimum(lowest, both)
            highest = both if highest is None else jnp.maximum(highest, both)
        idcol = jnp.concatenate(idcols, axis=0)
        every = idm[...]
        below = jnp.sum(jnp.where(every < jnp.min(lowest), 1.0, 0.0)).astype(jnp.int32)
        upto = jnp.sum(jnp.where(every <= jnp.max(highest), 1.0, 0.0)).astype(jnp.int32)
        start = below // TOK
        extent = upto - start * TOK
        n_large = (extent + (LARGE - 1 - MIDDLE - SMALL)) // LARGE
        extent = jnp.maximum(extent - n_large * LARGE, 0)
        n_middle = (extent + (MIDDLE - 1 - SMALL)) // MIDDLE
        n_small = (jnp.maximum(extent - n_middle * MIDDLE, 0) + (SMALL - 1)) // SMALL

        qdt = qd.T
        other = jnp.where((feature_q != idcol) & (feature_q < HEADS + 1), MASK, 0.0)
        qxt_f = jnp.where(lane_q < HEAD_DIM, qd * 0.125, other).T
        norms = jnp.sum(qxt_f[:HEAD_DIM] * qxt_f[:HEAD_DIM], axis=0, keepdims=True)
        small = jnp.max(norms) * key_norm < 1600.0

        def steps(step, state, wanted=True):
            def run(first, size):
                def body(n, state):
                    base = first + n * size
                    return step(
                        [
                            pl.ds(pl.multiple_of(base + t * SUB, TOK), SUB)
                            for t in range(size // SUB)
                        ],
                        state,
                    )

                return body

            first = start * TOK
            for size, count in ((LARGE, n_large), (MIDDLE, n_middle), (SMALL, n_small)):
                state = lax.fori_loop(0, jnp.where(wanted, count, 0), run(first, size), state)
                first = first + count * size
            return state

        def largest_step(tiles, top):
            for rows in tiles:
                s = dot_nn(kx[rows, :], qxt_f.astype(BF16))
                for r in range(0, SUB, 8):
                    top = jnp.maximum(top, s[r:r + 8])
            return top

        top = steps(largest_step, jnp.full((8, TQ), MASK, F32), ~small)
        top = jnp.where(small, 0.0, jnp.max(top, axis=0, keepdims=True))
        qxt = three(-top, HEAD_DIM + HEADS + 1, qxt_f)

        def value_step(tiles, ot):
            e = [jnp.exp(dot_nn(kx[rows, :], qxt)).astype(BF16) for rows in tiles]
            for n in range(0, len(tiles), 2):
                k = min(2, len(tiles) - n)
                rows = pl.ds(pl.multiple_of(tiles[n].start, TOK), k * SUB)
                ot = ot + dot_nn(kvt[HEAD_DIM:, rows], jnp.concatenate(e[n:n + k], axis=0))
            for rows, part in zip(tiles, e):
                sc[rows, :] = part
            return ot

        ot = steps(value_step, jnp.zeros((HEAD_DIM + 16, TQ), F32))
        inv = 1.0 / ot[HEAD_DIM:HEAD_DIM + 1]
        ot = (ot[:HEAD_DIM] * inv).astype(BF16).astype(F32)
        delta = jnp.sum(ot * qdt[HEAD_DIM:], axis=0, keepdims=True)
        gxt = three(-delta, 0, jnp.where(row_t < HEAD_DIM, 0.0, qdt))

        scaled = (qdt * inv).T
        right = jnp.concatenate(
            [
                jnp.where(lane_q < HEAD_DIM, scaled * 0.125, 0.0).astype(BF16),
                jnp.where(lane_q >= HEAD_DIM, scaled, 0.0).astype(BF16),
            ],
            axis=0,
        )

        def grad_step(tiles, dqt):
            e = [sc[rows, :] for rows in tiles]
            ds = [part * dot_nn(vx[rows, :], gxt).astype(BF16) for rows, part in zip(tiles, e)]
            for n in range(0, len(tiles), 2):
                k = min(2, len(tiles) - n)
                rows = pl.ds(pl.multiple_of(tiles[n].start, TOK), k * SUB)
                dqt = dqt + dot_nn(kvt[:HEAD_DIM, rows], jnp.concatenate(ds[n:n + k], axis=0))
            added = [
                acc[rows, :] + dot_nn(jnp.concatenate([a, b], axis=1), right)
                for rows, a, b in zip(tiles, ds, e)
            ]
            for rows, part in zip(tiles, added):
                acc[rows, :] = part
            return dqt

        dqt = steps(grad_step, jnp.zeros((HEAD_DIM, TQ), F32))
        both = jnp.concatenate([ot, dqt * (inv * 0.125)], axis=0).T.astype(BF16)
        for a in range(Q_SRC):
            send_ref[(c0 + a) % N_R, (c0 + a) // N_R, TOK:, :] = both[a * HALF:(a + 1) * HALF]
        return carry

    lax.fori_loop(0, N_QB, query_block, 0)

    def finish(c, carry):
        rows = pl.ds(pl.multiple_of(c * TOK, TOK), TOK)
        send_ref[c % N_R, c // N_R, :TOK, :] = acc[rows, :].astype(BF16)
        return carry

    lax.fori_loop(0, N_CTX, finish, 0, unroll=4)


def attend(recv):
    vmem = pl.BlockSpec(memory_space=pltpu.VMEM)
    padded = SEQ + LARGE
    return pl.pallas_call(
        attend_kernel,
        in_specs=[vmem],
        out_specs=vmem,
        out_shape=jax.ShapeDtypeStruct((N_R, N_X, OUT_ROWS, TOK), BF16),
        scratch_shapes=[
            pltpu.VMEM((padded, TOK), BF16),
            pltpu.VMEM((padded, TOK), BF16),
            pltpu.VMEM((TOK + 16, padded), BF16),
            pltpu.VMEM((N_CTX, TOK), F32),
            pltpu.VMEM((padded, TQ), BF16),
            pltpu.VMEM((padded, TOK), F32),
        ],
        compiler_params=pltpu.CompilerParams(vmem_limit_bytes=28 * MIB),
        cost_estimate=pl.CostEstimate(flops=25 * 10**9, bytes_accessed=4 * 10**6, transcendentals=0),
        name="attend",
    )(recv)


def unproject_kernel(me_ref, c0, c1, c2, c3, x_hbm, gain_hbm, wqkv_hbm, wo_hbm, out_ref, gx_ref, x_ref, gain_ref, wqkv, wo, sems, in_sems):
    copies = [
        fetch(wqkv_hbm, wo_hbm, wqkv, wo, sems, d, (me_ref[0] ^ d) * 256) for d in range(N_X)
    ]
    for group in copies:
        for copy in group:
            copy.start()
    inputs = [
        pltpu.make_async_copy(x_hbm, x_ref, in_sems.at[0]),
        pltpu.make_async_copy(gain_hbm, gain_ref, in_sems.at[1]),
    ]
    for copy in inputs:
        copy.start()
    result = jnp.zeros((TOK, D), F32)
    g = jnp.zeros((TOK, D), F32)
    for d, ref in enumerate((c0, c1, c2, c3)):
        for copy in copies[d]:
            copy.wait()
        result = result + dot_nn(ref[:, 768:], wo[d])
        for m in range(3):
            g = g + dot_nt(ref[:, m * 256:(m + 1) * 256], wqkv[d, m])
    out_ref[...] = result.astype(BF16)
    for copy in inputs:
        copy.wait()
    x = x_ref[...].astype(F32)
    cen = x - jnp.mean(x, axis=1, keepdims=True)
    inv = lax.rsqrt(jnp.mean(cen * cen, axis=1, keepdims=True) + EPSILON)
    x_hat = cen * inv
    g = g * gain_ref[...]
    gx = inv * (
        g - jnp.mean(g, axis=1, keepdims=True) - x_hat * jnp.mean(g * x_hat, axis=1, keepdims=True)
    )
    gx_ref[...] = gx.astype(BF16)


def unproject(me, pieces, x, gain, w_qkv, w_out):
    vmem = pl.BlockSpec(memory_space=pltpu.VMEM)
    hbm = pl.BlockSpec(memory_space=pltpu.HBM)
    return pl.pallas_call(
        unproject_kernel,
        in_specs=[pl.BlockSpec(memory_space=pltpu.SMEM)] + [vmem] * 4 + [hbm] * 4,
        out_specs=[vmem] * 2,
        out_shape=[jax.ShapeDtypeStruct((TOK, D), BF16)] * 2,
        scratch_shapes=[
            pltpu.VMEM((TOK, D), BF16),
            pltpu.VMEM((1, D), F32),
            *FETCHED,
            pltpu.SemaphoreType.DMA((2,)),
        ],
        compiler_params=pltpu.CompilerParams(vmem_limit_bytes=56 * MIB),
        cost_estimate=pl.CostEstimate(flops=7 * 10**9, bytes_accessed=10**7, transcendentals=0),
        name="unproject",
    )(me, *pieces, x, gain, w_qkv, w_out)


def repack_kernel(me_ref, recv_ref, *cols_refs):
    for d, cols_ref in enumerate(cols_refs):
        at = me_ref[0] ^ d
        parts = [[], [], [], []]
        for h in range(4):
            lo, hi = recv_ref[2 * h, at].astype(F32), recv_ref[2 * h + 1, at].astype(F32)
            kv = lo[:TOK] + hi[:TOK]
            aq = jnp.concatenate([lo[TOK:], hi[TOK:]], axis=0)
            parts[0].append(aq[:, HEAD_DIM:])
            parts[1].append(kv[:, :HEAD_DIM])
            parts[2].append(kv[:, HEAD_DIM:])
            parts[3].append(aq[:, :HEAD_DIM])
        for n, part in enumerate(parts):
            cols_ref[:, n * 256:(n + 1) * 256] = jnp.concatenate(part, axis=1).astype(BF16)


def repack(me, recv):
    vmem = pl.BlockSpec(memory_space=pltpu.VMEM)
    return pl.pallas_call(
        repack_kernel,
        in_specs=[pl.BlockSpec(memory_space=pltpu.SMEM), vmem],
        out_specs=[vmem] * N_X,
        out_shape=[jax.ShapeDtypeStruct((TOK, D), BF16)] * N_X,
        compiler_params=pltpu.CompilerParams(vmem_limit_bytes=16 * MIB),
        name="repack",
    )(me, recv)


def weights_kernel(me_ref, c0, c1, c2, c3, b0, b1, b2, b3, own_ref, other_ref):
    cols_refs = (c0, c1, c2, c3)
    cols = jnp.concatenate([ref[...] for ref in cols_refs], axis=0)
    both = jnp.concatenate([b0[...], b1[...], b2[...], b3[...]], axis=0)
    first_core = me_ref[1] == 0
    for zl in range(2):
        parts = []
        for m in (2 * zl, 2 * zl + 1):
            left = dot_tn(both[:, m * 256:(m + 1) * 256], cols[:, :768])
            right = dot_tn(cols[:, 768:], both[:, D + m * 256:D + (m + 1) * 256])
            parts.append((left, right))
        for n in range(2):
            cols_of = slice(0, 768) if n == 0 else slice(768, D)
            own = jnp.where(first_core, parts[0][n], parts[1][n]).astype(BF16)
            other = jnp.where(first_core, parts[1][n], parts[0][n]).astype(BF16)
            for r in range(N_R):
                own_ref[8 * zl + r, :, cols_of] = own[32 * r:32 * r + 32]
                other_ref[8 * zl + r, :, cols_of] = other[32 * r:32 * r + 32]


def weights(me, cols, both):
    vmem = pl.BlockSpec(memory_space=pltpu.VMEM)
    return pl.pallas_call(
        weights_kernel,
        in_specs=[pl.BlockSpec(memory_space=pltpu.SMEM)] + [vmem] * 8,
        out_specs=[vmem] * 2,
        out_shape=[jax.ShapeDtypeStruct((N_CTX // 2, 32, D), BF16)] * 2,
        cost_estimate=pl.CostEstimate(flops=2 * 10**9, bytes_accessed=4 * 10**6, transcendentals=0),
        compiler_params=pltpu.CompilerParams(vmem_limit_bytes=24 * MIB),
        name="weights",
    )(me, *cols, *both)


def assemble_kernel(me_ref, a_ref, b_ref, c_ref, d_ref, qkv_ref, out_ref):
    for d, ref in enumerate((a_ref, b_ref, c_ref, d_ref)):
        start = (me_ref[0] ^ d) * 256
        part = ref[...].astype(F32)
        for n in range(3):
            cols = pl.ds(pl.multiple_of(start + n * D, 256), 256)
            qkv_ref[:, cols] = part[:, n * 256:(n + 1) * 256]
        out_ref[:, pl.ds(pl.multiple_of(start, 256), 256)] = part[:, 768:]


def assemble(me, parts):
    vmem = pl.BlockSpec(memory_space=pltpu.VMEM)
    return pl.pallas_call(
        assemble_kernel,
        in_specs=[pl.BlockSpec(memory_space=pltpu.SMEM)] + [vmem] * 4,
        out_specs=[vmem] * 2,
        out_shape=[jax.ShapeDtypeStruct((32, 3 * D), F32), jax.ShapeDtypeStruct((32, D), F32)],
        compiler_params=pltpu.CompilerParams(vmem_limit_bytes=8 * MIB),
        name="assemble",
    )(me, *parts)


def swap(piece, axis, d):
    return piece if d == 0 else lax.ppermute(piece, axis, [(i, i ^ d) for i in range(4)])


def shards(patches, gain, w_qkv, w_out, image_ids, grad_out):
    x, cot = patches[0], grad_out[0]
    gain_row = gain[None]
    me = jnp.stack([lax.axis_index("x"), lax.axis_index("core")]).astype(jnp.int32)
    me_grp = lax.axis_index(("zl", "core")).astype(jnp.int32)[None]
    send, both = project(x, cot, gain_row, image_ids, w_qkv, w_out)
    recv = lax.all_to_all(send, ("x", "r"), 0, 0, tiled=True)
    recv, both = lax.optimization_barrier((recv, both))
    both = [swap(both, "x", d) for d in range(N_X)]
    done, both, me, me_grp = lax.optimization_barrier((attend(recv), both, me, me_grp))
    back = lax.all_to_all(done, "r", 0, 0, tiled=True)
    cols = repack(me, back)
    own, other = weights(me, cols, both)
    got = lax.ppermute(other, "core", [(0, 1), (1, 0)])
    cols = [swap(cols[d], "x", d) for d in range(N_X)]
    terms = (own.astype(F32) + got.astype(F32)).astype(BF16)
    parts = lax.all_to_all(terms, ("zl", "r"), 0, 0, tiled=True)
    out, grad_x = unproject(me, cols, x, gain_row, w_qkv, w_out)
    factor = 1.0 / math.sqrt(N_GRP * SEQ)
    share = (jnp.sum(parts.astype(F32), axis=0) * factor).astype(BF16)
    flip = [(s * N_X + j, j * N_X + s) for s in range(N_GRP) for j in range(N_X)]
    share_qkv = lax.ppermute(share[:, :768], ("zl", "core", "x"), flip)
    share = jnp.concatenate([share_qkv, share[:, 768:]], axis=1)
    shares = [swap(share, ("zl", "core"), d) for d in range(N_GRP)]
    grad_qkv, grad_w_out = assemble(me_grp, shares)
    return out[None], grad_x[None], grad_qkv, grad_w_out


def solution(mesh):
    fine = Mesh(mesh.devices.reshape(2, 2, N_X, N_R), ("zl", "core", "x", "r"))
    grp, ctx = ("zl", "core"), ("x", "r")
    in_specs = (P(grp, ctx, None), P(), P(), P(), P(grp, ctx), P(grp, ctx, None))
    out_specs = (P(grp, ctx, None), P(grp, ctx, None), P(ctx, None), P(ctx, None))
    return jax.shard_map(shards, mesh=fine, in_specs=in_specs, out_specs=out_specs, check_vma=False)
```

```python
import functools
import math

import jax
import jax.numpy as jnp
from jax import lax
from jax.experimental import pallas as pl
from jax.experimental.pallas import tpu as pltpu
from jax.sharding import Mesh, PartitionSpec as P

HEADS = 16
HEAD_DIM = 64
D = HEADS * HEAD_DIM
TOK = 128
HALF = TOK // 2
N_CTX = 32
N_GRP = 4
N_X = 4
N_R = 8
SEQ = TOK * N_CTX
ID_ROWS = 16
IN_ROWS = TOK + HALF + ID_ROWS
OUT_ROWS = TOK + HALF
TQ = 256
LARGE, MIDDLE, SMALL = 2176, 896, 384
SUB = 128
Q_SRC = TQ // HALF
N_QB = N_CTX // Q_SRC
EPSILON = 1e-06
MASK = -1e30
MIB = 1024 * 1024
F32 = jnp.float32
BF16 = jnp.bfloat16


def dot_nn(a, b):
    return jnp.dot(a, b, preferred_element_type=F32)


def dot_nt(a, b):
    return lax.dot_general(a, b, (((1,), (1,)), ((), ())), preferred_element_type=F32)


def dot_tn(a, b):
    return lax.dot_general(a, b, (((0,), (0,)), ((), ())), preferred_element_type=F32)


def lanes(shape):
    return lax.broadcasted_iota(jnp.int32, shape, 1)


def fetch(wqkv_hbm, wo_hbm, wqkv, wo, sems, n, start):
    start = start if isinstance(start, int) else pl.multiple_of(start, 256)
    copies = [pltpu.make_async_copy(wo_hbm.at[pl.ds(start, 256), :], wo.at[n], sems.at[n, 3])]
    for m in range(3):
        cols = pl.ds(start + m * D, 256)
        copies.append(pltpu.make_async_copy(wqkv_hbm.at[:, cols], wqkv.at[n, m], sems.at[n, m]))
    return copies


FETCHED = [
    pltpu.VMEM((4, 3, D, 256), BF16),
    pltpu.VMEM((4, 256, D), BF16),
    pltpu.SemaphoreType.DMA((4, 4)),
]


def project_kernel(x_hbm, cot_hbm, gain_hbm, ids_hbm, wqkv_hbm, wo_hbm, send_ref, both_ref, x_ref, gain_ref, ids_ref, wqkv, wo, sems, in_sems):
    cot_ref = both_ref.at[:, D:]
    arrays = ((x_hbm, x_ref), (gain_hbm, gain_ref), (ids_hbm, ids_ref), (cot_hbm, cot_ref))
    inputs = [pltpu.make_async_copy(*pair, in_sems.at[n]) for n, pair in enumerate(arrays)]
    copies = [fetch(wqkv_hbm, wo_hbm, wqkv, wo, sems, n, n * 256) for n in range(4)]
    for copy in inputs + copies[0]:
        copy.start()
    for copy in inputs[:3]:
        copy.wait()
    for group in copies[1:]:
        for copy in group:
            copy.start()
    x = x_ref[...].astype(F32)
    cen = x - jnp.mean(x, axis=1, keepdims=True)
    inv = lax.rsqrt(jnp.mean(cen * cen, axis=1, keepdims=True) + EPSILON)
    n = (cen * inv * gain_ref[...]).astype(BF16)
    both_ref[:, :D] = n
    ids = ids_ref[...].astype(F32)
    rolled = jnp.concatenate([ids[:, HALF:], ids[:, :HALF]], axis=1)
    inputs[3].wait()
    for j in range(4):
        for copy in copies[j]:
            copy.wait()
        g = dot_nt(cot_ref[...], wo[j])
        q, k, v = (dot_nn(n, wqkv[j, m]) for m in range(3))
        for h in range(4):
            cols = slice(h * HEAD_DIM, (h + 1) * HEAD_DIM)
            kv = jnp.concatenate([k[:, cols], v[:, cols]], axis=1).astype(BF16)
            qg = jnp.concatenate([q[:, cols], g[:, cols]], axis=1).astype(BF16)
            for p in range(2):
                own = ids if p == 0 else rolled
                rows = jnp.concatenate(
                    [jnp.broadcast_to(ids, (8, TOK)), jnp.broadcast_to(own, (8, TOK))], axis=0
                )
                to = 8 * j + 2 * h + p
                send_ref[to, :TOK, :] = kv
                send_ref[to, TOK:OUT_ROWS, :] = qg[p * HALF:(p + 1) * HALF, :]
                send_ref[to, OUT_ROWS:, :] = rows.astype(BF16)


def project(x, cot, gain, ids, w_qkv, w_out):
    vmem = pl.BlockSpec(memory_space=pltpu.VMEM)
    hbm = pl.BlockSpec(memory_space=pltpu.HBM)
    return pl.pallas_call(
        project_kernel,
        in_specs=[hbm] * 6,
        out_specs=[vmem] * 2,
        out_shape=[
            jax.ShapeDtypeStruct((N_CTX, IN_ROWS, TOK), BF16),
            jax.ShapeDtypeStruct((TOK, 2 * D), BF16),
        ],
        scratch_shapes=[
            pltpu.VMEM((TOK, D), BF16),
            pltpu.VMEM((1, D), F32),
            pltpu.VMEM((1, TOK), jnp.int32),
            *FETCHED,
            pltpu.SemaphoreType.DMA((4,)),
        ],
        compiler_params=pltpu.CompilerParams(vmem_limit_bytes=56 * MIB),
        name="project",
    )(x, cot, gain, ids, w_qkv, w_out)


def attend_kernel(recv_ref, send_ref, kx, vx, kvt, idm, sc, acc):
    lane = lanes((TOK, TOK))
    feature = lane.astype(F32) - HEAD_DIM

    def prepare(c, largest):
        kv = recv_ref[c, :TOK, :].astype(F32)
        idrow = recv_ref[c, OUT_ROWS:, :].astype(F32)[:1]
        idm[pl.ds(c, 1), :] = idrow
        idcol = jnp.broadcast_to(idrow, (TOK, TOK)).T
        extra = jnp.where((feature == idcol) | ((feature > HEADS) & (feature < HEADS + 4)), 1.0, 0.0)
        rows = pl.ds(pl.multiple_of(c * TOK, TOK), TOK)
        kx[rows, :] = jnp.where(lane < HEAD_DIM, kv, extra).astype(BF16)
        vx[rows, :] = jnp.where(lane < HEAD_DIM, jnp.where(lane < 3, 1.0, 0.0), kv).astype(BF16)
        flipped = kv.T
        kvt[:TOK, rows] = flipped.astype(BF16)
        kvt[TOK:, rows] = jnp.ones((16, TOK), BF16)
        acc[rows, :] = jnp.zeros((TOK, TOK), F32)
        norm = jnp.sum(flipped[:HEAD_DIM] * flipped[:HEAD_DIM], axis=0, keepdims=True)
        return jnp.maximum(largest, norm)

    largest = lax.fori_loop(0, N_CTX, prepare, jnp.zeros((1, TOK), F32), unroll=4)
    key_norm = jnp.max(largest)
    for c in range(N_CTX, (SEQ + LARGE) // TOK):
        rows = slice(c * TOK, (c + 1) * TOK)
        kx[rows, :] = jnp.where(feature == HEADS, 1.0, 0.0).astype(BF16)
        vx[rows, :] = jnp.zeros((TOK, TOK), BF16)
        kvt[:, rows] = jnp.zeros((TOK + 16, TOK), BF16)

    lane_q = lanes((TQ, TOK))
    feature_q = lane_q.astype(F32) - HEAD_DIM
    row_t = lax.broadcasted_iota(jnp.int32, (TOK, TQ), 0)

    def three(row, start, rest):
        hi = row.astype(BF16).astype(F32)
        mid = (row - hi).astype(BF16).astype(F32)
        low = row - hi - mid
        for n, part in enumerate((hi, mid, low)):
            rest = jnp.where(row_t == start + n, part, rest)
        return rest.astype(BF16)

    def query_block(i, carry):
        c0 = i * Q_SRC
        qd = recv_ref[pl.ds(c0, Q_SRC), TOK:OUT_ROWS, :].reshape(TQ, TOK).astype(F32)
        idcols = []
        lowest, highest = None, None
        for a in range(Q_SRC):
            both = recv_ref[c0 + a, OUT_ROWS:, :].astype(F32)
            idcols.append(jnp.broadcast_to(both[8:9], (TOK, TOK)).T[:HALF])
            lowest = both if lowest is None else jnp.minimum(lowest, both)
            highest = both if highest is None else jnp.maximum(highest, both)
        idcol = jnp.concatenate(idcols, axis=0)
        every = idm[...]
        below = jnp.sum(jnp.where(every < jnp.min(lowest), 1.0, 0.0)).astype(jnp.int32)
        upto = jnp.sum(jnp.where(every <= jnp.max(highest), 1.0, 0.0)).astype(jnp.int32)
        start = below // TOK
        extent = upto - start * TOK
        n_large = (extent + (LARGE - 1 - MIDDLE - SMALL)) // LARGE
        extent = jnp.maximum(extent - n_large * LARGE, 0)
        n_middle = (extent + (MIDDLE - 1 - SMALL)) // MIDDLE
        n_small = (jnp.maximum(extent - n_middle * MIDDLE, 0) + (SMALL - 1)) // SMALL

        qdt = qd.T
        other = jnp.where((feature_q != idcol) & (feature_q < HEADS + 1), MASK, 0.0)
        qxt_f = jnp.where(lane_q < HEAD_DIM, qd * 0.125, other).T
        norms = jnp.sum(qxt_f[:HEAD_DIM] * qxt_f[:HEAD_DIM], axis=0, keepdims=True)
        small = jnp.max(norms) * key_norm < 1600.0

        def steps(step, state, wanted=True):
            def run(first, size):
                def body(n, state):
                    base = first + n * size
                    return step(
                        [
                            pl.ds(pl.multiple_of(base + t * SUB, TOK), SUB)
                            for t in range(size // SUB)
                        ],
                        state,
                    )

                return body

            first = start * TOK
            for size, count in ((LARGE, n_large), (MIDDLE, n_middle), (SMALL, n_small)):
                state = lax.fori_loop(0, jnp.where(wanted, count, 0), run(first, size), state)
                first = first + count * size
            return state

        def largest_step(tiles, top):
            for rows in tiles:
                s = dot_nn(kx[rows, :], qxt_f.astype(BF16))
                for r in range(0, SUB, 8):
                    top = jnp.maximum(top, s[r:r + 8])
            return top

        top = steps(largest_step, jnp.full((8, TQ), MASK, F32), ~small)
        top = jnp.where(small, 0.0, jnp.max(top, axis=0, keepdims=True))
        qxt = three(-top, HEAD_DIM + HEADS + 1, qxt_f)

        def value_step(tiles, ot):
            e = [jnp.exp(dot_nn(kx[rows, :], qxt)).astype(BF16) for rows in tiles]
            for n in range(0, len(tiles), 2):
                k = min(2, len(tiles) - n)
                rows = pl.ds(pl.multiple_of(tiles[n].start, TOK), k * SUB)
                ot = ot + dot_nn(kvt[HEAD_DIM:, rows], jnp.concatenate(e[n:n + k], axis=0))
            for rows, part in zip(tiles, e):
                sc[rows, :] = part
            return ot

        ot = steps(value_step, jnp.zeros((HEAD_DIM + 16, TQ), F32))
        inv = 1.0 / ot[HEAD_DIM:HEAD_DIM + 1]
        ot = (ot[:HEAD_DIM] * inv).astype(BF16).astype(F32)
        delta = jnp.sum(ot * qdt[HEAD_DIM:], axis=0, keepdims=True)
        gxt = three(-delta, 0, jnp.where(row_t < HEAD_DIM, 0.0, qdt))

        scaled = (qdt * inv).T
        right = jnp.concatenate(
            [
                jnp.where(lane_q < HEAD_DIM, scaled * 0.125, 0.0).astype(BF16),
                jnp.where(lane_q >= HEAD_DIM, scaled, 0.0).astype(BF16),
            ],
            axis=0,
        )

        def grad_step(tiles, dqt):
            e = [sc[rows, :] for rows in tiles]
            ds = [part * dot_nn(vx[rows, :], gxt).astype(BF16) for rows, part in zip(tiles, e)]
            for n in range(0, len(tiles), 2):
                k = min(2, len(tiles) - n)
                rows = pl.ds(pl.multiple_of(tiles[n].start, TOK), k * SUB)
                dqt = dqt + dot_nn(kvt[:HEAD_DIM, rows], jnp.concatenate(ds[n:n + k], axis=0))
            added = [
                acc[rows, :] + dot_nn(jnp.concatenate([a, b], axis=1), right)
                for rows, a, b in zip(tiles, ds, e)
            ]
            for rows, part in zip(tiles, added):
                acc[rows, :] = part
            return dqt

        dqt = steps(grad_step, jnp.zeros((HEAD_DIM, TQ), F32))
        both = jnp.concatenate([ot, dqt * (inv * 0.125)], axis=0).T.astype(BF16)
        for a in range(Q_SRC):
            send_ref[(c0 + a) % N_R, (c0 + a) // N_R, TOK:, :] = both[a * HALF:(a + 1) * HALF]
        return carry

    lax.fori_loop(0, N_QB, query_block, 0)

    def finish(c, carry):
        rows = pl.ds(pl.multiple_of(c * TOK, TOK), TOK)
        send_ref[c % N_R, c // N_R, :TOK, :] = acc[rows, :].astype(BF16)
        return carry

    lax.fori_loop(0, N_CTX, finish, 0, unroll=4)


def attend(recv):
    vmem = pl.BlockSpec(memory_space=pltpu.VMEM)
    padded = SEQ + LARGE
    return pl.pallas_call(
        attend_kernel,
        in_specs=[vmem],
        out_specs=vmem,
        out_shape=jax.ShapeDtypeStruct((N_R, N_X, OUT_ROWS, TOK), BF16),
        scratch_shapes=[
            pltpu.VMEM((padded, TOK), BF16),
            pltpu.VMEM((padded, TOK), BF16),
            pltpu.VMEM((TOK + 16, padded), BF16),
            pltpu.VMEM((N_CTX, TOK), F32),
            pltpu.VMEM((padded, TQ), BF16),
            pltpu.VMEM((padded, TOK), F32),
        ],
        compiler_params=pltpu.CompilerParams(vmem_limit_bytes=28 * MIB),
        cost_estimate=pl.CostEstimate(flops=25 * 10**9, bytes_accessed=4 * 10**6, transcendentals=0),
        name="attend",
    )(recv)


def unproject_kernel(me_ref, c0, c1, c2, c3, x_hbm, gain_hbm, wqkv_hbm, wo_hbm, out_ref, gx_ref, x_ref, gain_ref, wqkv, wo, sems, in_sems):
    copies = [
        fetch(wqkv_hbm, wo_hbm, wqkv, wo, sems, d, (me_ref[0] ^ d) * 256) for d in range(N_X)
    ]
    for group in copies:
        for copy in group:
            copy.start()
    inputs = [
        pltpu.make_async_copy(x_hbm, x_ref, in_sems.at[0]),
        pltpu.make_async_copy(gain_hbm, gain_ref, in_sems.at[1]),
    ]
    for copy in inputs:
        copy.start()
    result = jnp.zeros((TOK, D), F32)
    g = jnp.zeros((TOK, D), F32)
    for d, ref in enumerate((c0, c1, c2, c3)):
        for copy in copies[d]:
            copy.wait()
        result = result + dot_nn(ref[:, 768:], wo[d])
        for m in range(3):
            g = g + dot_nt(ref[:, m * 256:(m + 1) * 256], wqkv[d, m])
    out_ref[...] = result.astype(BF16)
    for copy in inputs:
        copy.wait()
    x = x_ref[...].astype(F32)
    cen = x - jnp.mean(x, axis=1, keepdims=True)
    inv = lax.rsqrt(jnp.mean(cen * cen, axis=1, keepdims=True) + EPSILON)
    x_hat = cen * inv
    g = g * gain_ref[...]
    gx = inv * (
        g - jnp.mean(g, axis=1, keepdims=True) - x_hat * jnp.mean(g * x_hat, axis=1, keepdims=True)
    )
    gx_ref[...] = gx.astype(BF16)


def unproject(me, pieces, x, gain, w_qkv, w_out):
    vmem = pl.BlockSpec(memory_space=pltpu.VMEM)
    hbm = pl.BlockSpec(memory_space=pltpu.HBM)
    return pl.pallas_call(
        unproject_kernel,
        in_specs=[pl.BlockSpec(memory_space=pltpu.SMEM)] + [vmem] * 4 + [hbm] * 4,
        out_specs=[vmem] * 2,
        out_shape=[jax.ShapeDtypeStruct((TOK, D), BF16)] * 2,
        scratch_shapes=[
            pltpu.VMEM((TOK, D), BF16),
            pltpu.VMEM((1, D), F32),
            *FETCHED,
            pltpu.SemaphoreType.DMA((2,)),
        ],
        compiler_params=pltpu.CompilerParams(vmem_limit_bytes=52 * MIB),
        cost_estimate=pl.CostEstimate(flops=7 * 10**9, bytes_accessed=10**7, transcendentals=0),
        name="unproject",
    )(me, *pieces, x, gain, w_qkv, w_out)


def repack_kernel(me_ref, recv_ref, *cols_refs):
    for d, cols_ref in enumerate(cols_refs):
        at = me_ref[0] ^ d
        parts = [[], [], [], []]
        for h in range(4):
            lo, hi = recv_ref[2 * h, at].astype(F32), recv_ref[2 * h + 1, at].astype(F32)
            kv = lo[:TOK] + hi[:TOK]
            aq = jnp.concatenate([lo[TOK:], hi[TOK:]], axis=0)
            parts[0].append(aq[:, HEAD_DIM:])
            parts[1].append(kv[:, :HEAD_DIM])
            parts[2].append(kv[:, HEAD_DIM:])
            parts[3].append(aq[:, :HEAD_DIM])
        for n, part in enumerate(parts):
            cols_ref[:, n * 256:(n + 1) * 256] = jnp.concatenate(part, axis=1).astype(BF16)


def repack(me, recv):
    vmem = pl.BlockSpec(memory_space=pltpu.VMEM)
    return pl.pallas_call(
        repack_kernel,
        in_specs=[pl.BlockSpec(memory_space=pltpu.SMEM), vmem],
        out_specs=[vmem] * N_X,
        out_shape=[jax.ShapeDtypeStruct((TOK, D), BF16)] * N_X,
        compiler_params=pltpu.CompilerParams(vmem_limit_bytes=16 * MIB),
        name="repack",
    )(me, recv)


def weights_kernel(me_ref, c0, c1, c2, c3, b0, b1, b2, b3, own_ref, other_ref):
    cols_refs = (c0, c1, c2, c3)
    cols = jnp.concatenate([ref[...] for ref in cols_refs], axis=0)
    both = jnp.concatenate([b0[...], b1[...], b2[...], b3[...]], axis=0)
    first_core = me_ref[1] == 0
    for zl in range(2):
        parts = []
        for m in (2 * zl, 2 * zl + 1):
            left = dot_tn(both[:, m * 256:(m + 1) * 256], cols[:, :768])
            right = dot_tn(cols[:, 768:], both[:, D + m * 256:D + (m + 1) * 256])
            parts.append((left, right))
        for n in range(2):
            cols_of = slice(0, 768) if n == 0 else slice(768, D)
            own = jnp.where(first_core, parts[0][n], parts[1][n]).astype(BF16)
            other = jnp.where(first_core, parts[1][n], parts[0][n]).astype(BF16)
            for r in range(N_R):
                own_ref[8 * zl + r, :, cols_of] = own[32 * r:32 * r + 32]
                other_ref[8 * zl + r, :, cols_of] = other[32 * r:32 * r + 32]


def weights(me, cols, both):
    vmem = pl.BlockSpec(memory_space=pltpu.VMEM)
    return pl.pallas_call(
        weights_kernel,
        in_specs=[pl.BlockSpec(memory_space=pltpu.SMEM)] + [vmem] * 8,
        out_specs=[vmem] * 2,
        out_shape=[jax.ShapeDtypeStruct((N_CTX // 2, 32, D), BF16)] * 2,
        cost_estimate=pl.CostEstimate(flops=2 * 10**9, bytes_accessed=4 * 10**6, transcendentals=0),
        compiler_params=pltpu.CompilerParams(vmem_limit_bytes=24 * MIB),
        name="weights",
    )(me, *cols, *both)


def assemble_kernel(me_ref, a_ref, b_ref, c_ref, d_ref, qkv_ref, out_ref):
    for d, ref in enumerate((a_ref, b_ref, c_ref, d_ref)):
        start = (me_ref[0] ^ d) * 256
        part = ref[...].astype(F32)
        for n in range(3):
            cols = pl.ds(pl.multiple_of(start + n * D, 256), 256)
            qkv_ref[:, cols] = part[:, n * 256:(n + 1) * 256]
        out_ref[:, pl.ds(pl.multiple_of(start, 256), 256)] = part[:, 768:]


def assemble(me, parts):
    vmem = pl.BlockSpec(memory_space=pltpu.VMEM)
    return pl.pallas_call(
        assemble_kernel,
        in_specs=[pl.BlockSpec(memory_space=pltpu.SMEM)] + [vmem] * 4,
        out_specs=[vmem] * 2,
        out_shape=[jax.ShapeDtypeStruct((32, 3 * D), F32), jax.ShapeDtypeStruct((32, D), F32)],
        compiler_params=pltpu.CompilerParams(vmem_limit_bytes=8 * MIB),
        name="assemble",
    )(me, *parts)


def swap(piece, axis, d):
    return piece if d == 0 else lax.ppermute(piece, axis, [(i, i ^ d) for i in range(4)])


def shards(patches, gain, w_qkv, w_out, image_ids, grad_out):
    x, cot = patches[0], grad_out[0]
    gain_row = gain[None]
    me = jnp.stack([lax.axis_index("x"), lax.axis_index("core")]).astype(jnp.int32)
    me_grp = lax.axis_index(("zl", "core")).astype(jnp.int32)[None]
    send, both = project(x, cot, gain_row, image_ids, w_qkv, w_out)
    recv = lax.all_to_all(send, ("x", "r"), 0, 0, tiled=True)
    recv, both = lax.optimization_barrier((recv, both))
    both = [swap(both, "x", d) for d in range(N_X)]
    done, both, me, me_grp = lax.optimization_barrier((attend(recv), both, me, me_grp))
    back = lax.all_to_all(done, "r", 0, 0, tiled=True)
    cols = repack(me, back)
    own, other = weights(me, cols, both)
    got = lax.ppermute(other, "core", [(0, 1), (1, 0)])
    cols = [swap(cols[d], "x", d) for d in range(N_X)]
    terms = (own.astype(F32) + got.astype(F32)).astype(BF16)
    parts = lax.all_to_all(terms, ("zl", "r"), 0, 0, tiled=True)
    out, grad_x = unproject(me, cols, x, gain_row, w_qkv, w_out)
    factor = 1.0 / math.sqrt(N_GRP * SEQ)
    share = (jnp.sum(parts.astype(F32), axis=0) * factor).astype(BF16)
    flip = [(s * N_X + j, j * N_X + s) for s in range(N_GRP) for j in range(N_X)]
    share_qkv = lax.ppermute(share[:, :768], ("zl", "core", "x"), flip)
    share = jnp.concatenate([share_qkv, share[:, 768:]], axis=1)
    shares = [swap(share, ("zl", "core"), d) for d in range(N_GRP)]
    grad_qkv, grad_w_out = assemble(me_grp, shares)
    return out[None], grad_x[None], grad_qkv, grad_w_out


def solution(mesh):
    fine = Mesh(mesh.devices.reshape(2, 2, N_X, N_R), ("zl", "core", "x", "r"))
    grp, ctx = ("zl", "core"), ("x", "r")
    in_specs = (P(grp, ctx, None), P(), P(), P(), P(grp, ctx), P(grp, ctx, None))
    out_specs = (P(grp, ctx, None), P(grp, ctx, None), P(ctx, None), P(ctx, None))
    return jax.shard_map(shards, mesh=fine, in_specs=in_specs, out_specs=out_specs, check_vma=False)
```

```python
import functools
import math

import jax
import jax.numpy as jnp
from jax import lax
from jax.experimental import pallas as pl
from jax.experimental.pallas import tpu as pltpu
from jax.sharding import Mesh, PartitionSpec as P

HEADS = 16
HEAD_DIM = 64
D = HEADS * HEAD_DIM
TOK = 128
HALF = TOK // 2
N_CTX = 32
N_GRP = 4
N_X = 4
N_R = 8
SEQ = TOK * N_CTX
ID_ROWS = 16
IN_ROWS = TOK + HALF + ID_ROWS
OUT_ROWS = TOK + HALF
TQ = 256
LARGE, MIDDLE, SMALL = 2176, 896, 384
SUB = 128
Q_SRC = TQ // HALF
N_QB = N_CTX // Q_SRC
EPSILON = 1e-06
MASK = -1e30
MIB = 1024 * 1024
F32 = jnp.float32
BF16 = jnp.bfloat16


def dot_nn(a, b):
    return jnp.dot(a, b, preferred_element_type=F32)


def dot_nt(a, b):
    return lax.dot_general(a, b, (((1,), (1,)), ((), ())), preferred_element_type=F32)


def dot_tn(a, b):
    return lax.dot_general(a, b, (((0,), (0,)), ((), ())), preferred_element_type=F32)


def lanes(shape):
    return lax.broadcasted_iota(jnp.int32, shape, 1)


def fetch(wqkv_hbm, wo_hbm, wqkv, wo, sems, n, start):
    start = start if isinstance(start, int) else pl.multiple_of(start, 256)
    copies = [pltpu.make_async_copy(wo_hbm.at[pl.ds(start, 256), :], wo.at[n], sems.at[n, 3])]
    for m in range(3):
        cols = pl.ds(start + m * D, 256)
        copies.append(pltpu.make_async_copy(wqkv_hbm.at[:, cols], wqkv.at[n, m], sems.at[n, m]))
    return copies


FETCHED = [
    pltpu.VMEM((4, 3, D, 256), BF16),
    pltpu.VMEM((4, 256, D), BF16),
    pltpu.SemaphoreType.DMA((4, 4)),
]


def project_kernel(x_hbm, cot_hbm, gain_hbm, ids_hbm, wqkv_hbm, wo_hbm, send_ref, both_ref, x_ref, gain_ref, ids_ref, wqkv, wo, sems, in_sems):
    cot_ref = both_ref.at[:, D:]
    arrays = ((x_hbm, x_ref), (gain_hbm, gain_ref), (ids_hbm, ids_ref), (cot_hbm, cot_ref))
    inputs = [pltpu.make_async_copy(*pair, in_sems.at[n]) for n, pair in enumerate(arrays)]
    copies = [fetch(wqkv_hbm, wo_hbm, wqkv, wo, sems, n, n * 256) for n in range(4)]
    for copy in inputs + copies[0]:
        copy.start()
    for copy in inputs[:3]:
        copy.wait()
    for group in copies[1:]:
        for copy in group:
            copy.start()
    x = x_ref[...].astype(F32)
    cen = x - jnp.mean(x, axis=1, keepdims=True)
    inv = lax.rsqrt(jnp.mean(cen * cen, axis=1, keepdims=True) + EPSILON)
    n = (cen * inv * gain_ref[...]).astype(BF16)
    both_ref[:, :D] = n
    ids = ids_ref[...].astype(F32)
    rolled = jnp.concatenate([ids[:, HALF:], ids[:, :HALF]], axis=1)
    inputs[3].wait()
    for j in range(4):
        for copy in copies[j]:
            copy.wait()
        g = dot_nt(cot_ref[...], wo[j])
        q, k, v = (dot_nn(n, wqkv[j, m]) for m in range(3))
        for h in range(4):
            cols = slice(h * HEAD_DIM, (h + 1) * HEAD_DIM)
            kv = jnp.concatenate([k[:, cols], v[:, cols]], axis=1).astype(BF16)
            qg = jnp.concatenate([q[:, cols], g[:, cols]], axis=1).astype(BF16)
            for p in range(2):
                own = ids if p == 0 else rolled
                rows = jnp.concatenate(
                    [jnp.broadcast_to(ids, (8, TOK)), jnp.broadcast_to(own, (8, TOK))], axis=0
                )
                to = 8 * j + 2 * h + p
                send_ref[to, :TOK, :] = kv
                send_ref[to, TOK:OUT_ROWS, :] = qg[p * HALF:(p + 1) * HALF, :]
                send_ref[to, OUT_ROWS:, :] = rows.astype(BF16)


def project(x, cot, gain, ids, w_qkv, w_out):
    vmem = pl.BlockSpec(memory_space=pltpu.VMEM)
    hbm = pl.BlockSpec(memory_space=pltpu.HBM)
    return pl.pallas_call(
        project_kernel,
        in_specs=[hbm] * 6,
        out_specs=[vmem] * 2,
        out_shape=[
            jax.ShapeDtypeStruct((N_CTX, IN_ROWS, TOK), BF16),
            jax.ShapeDtypeStruct((TOK, 2 * D), BF16),
        ],
        scratch_shapes=[
            pltpu.VMEM((TOK, D), BF16),
            pltpu.VMEM((1, D), F32),
            pltpu.VMEM((1, TOK), jnp.int32),
            *FETCHED,
            pltpu.SemaphoreType.DMA((4,)),
        ],
        compiler_params=pltpu.CompilerParams(vmem_limit_bytes=56 * MIB),
        name="project",
    )(x, cot, gain, ids, w_qkv, w_out)


def attend_kernel(recv_ref, send_ref, kx, vx, kvt, idm, sc, acc):
    lane = lanes((TOK, TOK))
    feature = lane.astype(F32) - HEAD_DIM

    def prepare(c, largest):
        kv = recv_ref[c, :TOK, :].astype(F32)
        idrow = recv_ref[c, OUT_ROWS:, :].astype(F32)[:1]
        idm[pl.ds(c, 1), :] = idrow
        idcol = jnp.broadcast_to(idrow.astype(BF16), (TOK, TOK)).T.astype(F32)
        extra = jnp.where((feature == idcol) | ((feature > HEADS) & (feature < HEADS + 4)), 1.0, 0.0)
        rows = pl.ds(pl.multiple_of(c * TOK, TOK), TOK)
        kx[rows, :] = jnp.where(lane < HEAD_DIM, kv, extra).astype(BF16)
        vx[rows, :] = jnp.where(lane < HEAD_DIM, jnp.where(lane < 3, 1.0, 0.0), kv).astype(BF16)
        flipped = recv_ref[c, :TOK, :].T
        kvt[:TOK, rows] = flipped
        flipped = flipped.astype(F32)
        kvt[TOK:, rows] = jnp.ones((16, TOK), BF16)
        acc[rows, :] = jnp.zeros((TOK, TOK), F32)
        norm = jnp.sum(flipped[:HEAD_DIM] * flipped[:HEAD_DIM], axis=0, keepdims=True)
        return jnp.maximum(largest, norm)

    largest = lax.fori_loop(0, N_CTX, prepare, jnp.zeros((1, TOK), F32), unroll=8)
    key_norm = jnp.max(largest)
    for c in range(N_CTX, (SEQ + LARGE) // TOK):
        rows = slice(c * TOK, (c + 1) * TOK)
        kx[rows, :] = jnp.where(feature == HEADS, 1.0, 0.0).astype(BF16)
        vx[rows, :] = jnp.zeros((TOK, TOK), BF16)
        kvt[:, rows] = jnp.zeros((TOK + 16, TOK), BF16)

    lane_q = lanes((TQ, TOK))
    feature_q = lane_q.astype(F32) - HEAD_DIM
    row_t = lax.broadcasted_iota(jnp.int32, (TOK, TQ), 0)

    def three(row, start, rest):
        hi = row.astype(BF16).astype(F32)
        mid = (row - hi).astype(BF16).astype(F32)
        low = row - hi - mid
        for n, part in enumerate((hi, mid, low)):
            rest = jnp.where(row_t == start + n, part, rest)
        return rest.astype(BF16)

    def query_block(i, carry):
        c0 = i * Q_SRC
        qd = recv_ref[pl.ds(c0, Q_SRC), TOK:OUT_ROWS, :].reshape(TQ, TOK).astype(F32)
        idcols = []
        lowest, highest = None, None
        for a in range(Q_SRC):
            both = recv_ref[c0 + a, OUT_ROWS:, :].astype(F32)
            idcols.append(jnp.broadcast_to(both[8:9].astype(BF16), (TOK, TOK)).T[:HALF].astype(F32))
            lowest = both if lowest is None else jnp.minimum(lowest, both)
            highest = both if highest is None else jnp.maximum(highest, both)
        idcol = jnp.concatenate(idcols, axis=0)
        every = idm[...]
        below = jnp.sum(jnp.where(every < jnp.min(lowest), 1.0, 0.0)).astype(jnp.int32)
        upto = jnp.sum(jnp.where(every <= jnp.max(highest), 1.0, 0.0)).astype(jnp.int32)
        start = below // TOK
        extent = upto - start * TOK
        n_large = (extent + (LARGE - 1 - MIDDLE - SMALL)) // LARGE
        extent = jnp.maximum(extent - n_large * LARGE, 0)
        n_middle = (extent + (MIDDLE - 1 - SMALL)) // MIDDLE
        n_small = (jnp.maximum(extent - n_middle * MIDDLE, 0) + (SMALL - 1)) // SMALL

        qdt = qd.astype(BF16).T.astype(F32)
        other = jnp.where((feature_q != idcol) & (feature_q < HEADS + 1), MASK, 0.0)
        qxt_f = jnp.where(lane_q < HEAD_DIM, qd * 0.125, other).astype(BF16).T.astype(F32)
        norms = jnp.sum(qxt_f[:HEAD_DIM] * qxt_f[:HEAD_DIM], axis=0, keepdims=True)
        small = jnp.max(norms) * key_norm < 1600.0

        def steps(step, state, wanted=True):
            def run(first, size):
                def body(n, state):
                    base = first + n * size
                    return step(
                        [
                            pl.ds(pl.multiple_of(base + t * SUB, TOK), SUB)
                            for t in range(size // SUB)
                        ],
                        state,
                    )

                return body

            first = start * TOK
            for size, count in ((LARGE, n_large), (MIDDLE, n_middle), (SMALL, n_small)):
                state = lax.fori_loop(0, jnp.where(wanted, count, 0), run(first, size), state)
                first = first + count * size
            return state

        def largest_step(tiles, top):
            for rows in tiles:
                s = dot_nn(kx[rows, :], qxt_f.astype(BF16))
                for r in range(0, SUB, 8):
                    top = jnp.maximum(top, s[r:r + 8])
            return top

        top = steps(largest_step, jnp.full((8, TQ), MASK, F32), ~small)
        top = jnp.where(small, 0.0, jnp.max(top, axis=0, keepdims=True))
        qxt = three(-top, HEAD_DIM + HEADS + 1, qxt_f)

        def value_step(tiles, ot):
            e = [jnp.exp(dot_nn(kx[rows, :], qxt)).astype(BF16) for rows in tiles]
            for n in range(0, len(tiles), 2):
                k = min(2, len(tiles) - n)
                rows = pl.ds(pl.multiple_of(tiles[n].start, TOK), k * SUB)
                ot = ot + dot_nn(kvt[HEAD_DIM:, rows], jnp.concatenate(e[n:n + k], axis=0))
            for rows, part in zip(tiles, e):
                sc[rows, :] = part
            return ot

        ot = steps(value_step, jnp.zeros((HEAD_DIM + 16, TQ), F32))
        inv = 1.0 / ot[HEAD_DIM:HEAD_DIM + 1]
        ot = (ot[:HEAD_DIM] * inv).astype(BF16).astype(F32)
        delta = jnp.sum(ot * qdt[HEAD_DIM:], axis=0, keepdims=True)
        gxt = three(-delta, 0, jnp.where(row_t < HEAD_DIM, 0.0, qdt))

        scaled = (qdt * inv).T
        right = jnp.concatenate(
            [
                jnp.where(lane_q < HEAD_DIM, scaled * 0.125, 0.0).astype(BF16),
                jnp.where(lane_q >= HEAD_DIM, scaled, 0.0).astype(BF16),
            ],
            axis=0,
        )

        def grad_step(tiles, dqt):
            e = [sc[rows, :] for rows in tiles]
            ds = [part * dot_nn(vx[rows, :], gxt).astype(BF16) for rows, part in zip(tiles, e)]
            for n in range(0, len(tiles), 2):
                k = min(2, len(tiles) - n)
                rows = pl.ds(pl.multiple_of(tiles[n].start, TOK), k * SUB)
                dqt = dqt + dot_nn(kvt[:HEAD_DIM, rows], jnp.concatenate(ds[n:n + k], axis=0))
            added = [
                acc[rows, :] + dot_nn(jnp.concatenate([a, b], axis=1), right)
                for rows, a, b in zip(tiles, ds, e)
            ]
            for rows, part in zip(tiles, added):
                acc[rows, :] = part
            return dqt

        dqt = steps(grad_step, jnp.zeros((HEAD_DIM, TQ), F32))
        both = jnp.concatenate([ot, dqt * (inv * 0.125)], axis=0).T.astype(BF16)
        for a in range(Q_SRC):
            send_ref[(c0 + a) % N_R, (c0 + a) // N_R, TOK:, :] = both[a * HALF:(a + 1) * HALF]
        return carry

    lax.fori_loop(0, N_QB, query_block, 0)

    def finish(c, carry):
        rows = pl.ds(pl.multiple_of(c * TOK, TOK), TOK)
        send_ref[c % N_R, c // N_R, :TOK, :] = acc[rows, :].astype(BF16)
        return carry

    lax.fori_loop(0, N_CTX, finish, 0, unroll=8)


def attend(recv):
    vmem = pl.BlockSpec(memory_space=pltpu.VMEM)
    padded = SEQ + LARGE
    return pl.pallas_call(
        attend_kernel,
        in_specs=[vmem],
        out_specs=vmem,
        out_shape=jax.ShapeDtypeStruct((N_R, N_X, OUT_ROWS, TOK), BF16),
        scratch_shapes=[
            pltpu.VMEM((padded, TOK), BF16),
            pltpu.VMEM((padded, TOK), BF16),
            pltpu.VMEM((TOK + 16, padded), BF16),
            pltpu.VMEM((N_CTX, TOK), F32),
            pltpu.VMEM((padded, TQ), BF16),
            pltpu.VMEM((padded, TOK), F32),
        ],
        compiler_params=pltpu.CompilerParams(vmem_limit_bytes=28 * MIB),
        cost_estimate=pl.CostEstimate(flops=25 * 10**9, bytes_accessed=4 * 10**6, transcendentals=0),
        name="attend",
    )(recv)


def unproject_kernel(me_ref, c0, c1, c2, c3, x_hbm, gain_hbm, wqkv_hbm, wo_hbm, out_ref, gx_ref, x_ref, gain_ref, wqkv, wo, sems, in_sems):
    copies = [
        fetch(wqkv_hbm, wo_hbm, wqkv, wo, sems, d, (me_ref[0] ^ d) * 256) for d in range(N_X)
    ]
    for group in copies:
        for copy in group:
            copy.start()
    inputs = [
        pltpu.make_async_copy(x_hbm, x_ref, in_sems.at[0]),
        pltpu.make_async_copy(gain_hbm, gain_ref, in_sems.at[1]),
    ]
    for copy in inputs:
        copy.start()
    result = jnp.zeros((TOK, D), F32)
    g = jnp.zeros((TOK, D), F32)
    for d, ref in enumerate((c0, c1, c2, c3)):
        for copy in copies[d]:
            copy.wait()
        result = result + dot_nn(ref[:, 768:], wo[d])
        for m in range(3):
            g = g + dot_nt(ref[:, m * 256:(m + 1) * 256], wqkv[d, m])
    out_ref[...] = result.astype(BF16)
    for copy in inputs:
        copy.wait()
    x = x_ref[...].astype(F32)
    cen = x - jnp.mean(x, axis=1, keepdims=True)
    inv = lax.rsqrt(jnp.mean(cen * cen, axis=1, keepdims=True) + EPSILON)
    x_hat = cen * inv
    g = g * gain_ref[...]
    gx = inv * (
        g - jnp.mean(g, axis=1, keepdims=True) - x_hat * jnp.mean(g * x_hat, axis=1, keepdims=True)
    )
    gx_ref[...] = gx.astype(BF16)


def unproject(me, pieces, x, gain, w_qkv, w_out):
    vmem = pl.BlockSpec(memory_space=pltpu.VMEM)
    hbm = pl.BlockSpec(memory_space=pltpu.HBM)
    return pl.pallas_call(
        unproject_kernel,
        in_specs=[pl.BlockSpec(memory_space=pltpu.SMEM)] + [vmem] * 4 + [hbm] * 4,
        out_specs=[vmem] * 2,
        out_shape=[jax.ShapeDtypeStruct((TOK, D), BF16)] * 2,
        scratch_shapes=[
            pltpu.VMEM((TOK, D), BF16),
            pltpu.VMEM((1, D), F32),
            *FETCHED,
            pltpu.SemaphoreType.DMA((2,)),
        ],
        compiler_params=pltpu.CompilerParams(vmem_limit_bytes=52 * MIB),
        cost_estimate=pl.CostEstimate(flops=7 * 10**9, bytes_accessed=10**7, transcendentals=0),
        name="unproject",
    )(me, *pieces, x, gain, w_qkv, w_out)


def repack_kernel(me_ref, recv_ref, *cols_refs):
    for d, cols_ref in enumerate(cols_refs):
        at = me_ref[0] ^ d
        parts = [[], [], [], []]
        for h in range(4):
            lo, hi = recv_ref[2 * h, at].astype(F32), recv_ref[2 * h + 1, at].astype(F32)
            kv = lo[:TOK] + hi[:TOK]
            aq = jnp.concatenate([lo[TOK:], hi[TOK:]], axis=0)
            parts[0].append(aq[:, HEAD_DIM:])
            parts[1].append(kv[:, :HEAD_DIM])
            parts[2].append(kv[:, HEAD_DIM:])
            parts[3].append(aq[:, :HEAD_DIM])
        for n, part in enumerate(parts):
            cols_ref[:, n * 256:(n + 1) * 256] = jnp.concatenate(part, axis=1).astype(BF16)


def repack(me, recv):
    vmem = pl.BlockSpec(memory_space=pltpu.VMEM)
    return pl.pallas_call(
        repack_kernel,
        in_specs=[pl.BlockSpec(memory_space=pltpu.SMEM), vmem],
        out_specs=[vmem] * N_X,
        out_shape=[jax.ShapeDtypeStruct((TOK, D), BF16)] * N_X,
        compiler_params=pltpu.CompilerParams(vmem_limit_bytes=16 * MIB),
        name="repack",
    )(me, recv)


def weights_kernel(me_ref, c0, c1, c2, c3, b0, b1, b2, b3, own_ref, other_ref):
    cols_refs = (c0, c1, c2, c3)
    cols = jnp.concatenate([ref[...] for ref in cols_refs], axis=0)
    both = jnp.concatenate([b0[...], b1[...], b2[...], b3[...]], axis=0)
    first_core = me_ref[1] == 0
    for zl in range(2):
        parts = []
        for m in (2 * zl, 2 * zl + 1):
            left = dot_tn(both[:, m * 256:(m + 1) * 256], cols[:, :768])
            right = dot_tn(cols[:, 768:], both[:, D + m * 256:D + (m + 1) * 256])
            parts.append((left, right))
        for n in range(2):
            cols_of = slice(0, 768) if n == 0 else slice(768, D)
            own = jnp.where(first_core, parts[0][n], parts[1][n]).astype(BF16)
            other = jnp.where(first_core, parts[1][n], parts[0][n]).astype(BF16)
            for r in range(N_R):
                own_ref[8 * zl + r, :, cols_of] = own[32 * r:32 * r + 32]
                other_ref[8 * zl + r, :, cols_of] = other[32 * r:32 * r + 32]


def weights(me, cols, both):
    vmem = pl.BlockSpec(memory_space=pltpu.VMEM)
    return pl.pallas_call(
        weights_kernel,
        in_specs=[pl.BlockSpec(memory_space=pltpu.SMEM)] + [vmem] * 8,
        out_specs=[vmem] * 2,
        out_shape=[jax.ShapeDtypeStruct((N_CTX // 2, 32, D), BF16)] * 2,
        cost_estimate=pl.CostEstimate(flops=2 * 10**9, bytes_accessed=4 * 10**6, transcendentals=0),
        compiler_params=pltpu.CompilerParams(vmem_limit_bytes=24 * MIB),
        name="weights",
    )(me, *cols, *both)


def assemble_kernel(me_ref, a_ref, b_ref, c_ref, d_ref, qkv_ref, out_ref):
    for d, ref in enumerate((a_ref, b_ref, c_ref, d_ref)):
        start = (me_ref[0] ^ d) * 256
        part = ref[...].astype(F32)
        for n in range(3):
            cols = pl.ds(pl.multiple_of(start + n * D, 256), 256)
            qkv_ref[:, cols] = part[:, n * 256:(n + 1) * 256]
        out_ref[:, pl.ds(pl.multiple_of(start, 256), 256)] = part[:, 768:]


def assemble(me, parts):
    vmem = pl.BlockSpec(memory_space=pltpu.VMEM)
    return pl.pallas_call(
        assemble_kernel,
        in_specs=[pl.BlockSpec(memory_space=pltpu.SMEM)] + [vmem] * 4,
        out_specs=[vmem] * 2,
        out_shape=[jax.ShapeDtypeStruct((32, 3 * D), F32), jax.ShapeDtypeStruct((32, D), F32)],
        compiler_params=pltpu.CompilerParams(vmem_limit_bytes=8 * MIB),
        name="assemble",
    )(me, *parts)


def swap(piece, axis, d):
    return piece if d == 0 else lax.ppermute(piece, axis, [(i, i ^ d) for i in range(4)])


def shards(patches, gain, w_qkv, w_out, image_ids, grad_out):
    x, cot = patches[0], grad_out[0]
    gain_row = gain[None]
    me = jnp.stack([lax.axis_index("x"), lax.axis_index("core")]).astype(jnp.int32)
    me_grp = lax.axis_index(("zl", "core")).astype(jnp.int32)[None]
    send, both = project(x, cot, gain_row, image_ids, w_qkv, w_out)
    recv = lax.all_to_all(send, ("x", "r"), 0, 0, tiled=True)
    recv, both = lax.optimization_barrier((recv, both))
    both = [swap(both, "x", d) for d in range(N_X)]
    done, both, me, me_grp = lax.optimization_barrier((attend(recv), both, me, me_grp))
    back = lax.all_to_all(done, "r", 0, 0, tiled=True)
    cols = repack(me, back)
    own, other = weights(me, cols, both)
    got = lax.ppermute(other, "core", [(0, 1), (1, 0)])
    cols = [swap(cols[d], "x", d) for d in range(N_X)]
    terms = (own.astype(F32) + got.astype(F32)).astype(BF16)
    parts = lax.all_to_all(terms, ("zl", "r"), 0, 0, tiled=True)
    out, grad_x = unproject(me, cols, x, gain_row, w_qkv, w_out)
    factor = 1.0 / math.sqrt(N_GRP * SEQ)
    share = (jnp.sum(parts.astype(F32), axis=0) * factor).astype(BF16)
    flip = [(s * N_X + j, j * N_X + s) for s in range(N_GRP) for j in range(N_X)]
    share_qkv = lax.ppermute(share[:, :768], ("zl", "core", "x"), flip)
    share = jnp.concatenate([share_qkv, share[:, 768:]], axis=1)
    shares = [swap(share, ("zl", "core"), d) for d in range(N_GRP)]
    grad_qkv, grad_w_out = assemble(me_grp, shares)
    return out[None], grad_x[None], grad_qkv, grad_w_out


def solution(mesh):
    fine = Mesh(mesh.devices.reshape(2, 2, N_X, N_R), ("zl", "core", "x", "r"))
    grp, ctx = ("zl", "core"), ("x", "r")
    in_specs = (P(grp, ctx, None), P(), P(), P(), P(grp, ctx), P(grp, ctx, None))
    out_specs = (P(grp, ctx, None), P(grp, ctx, None), P(ctx, None), P(ctx, None))
    return jax.shard_map(shards, mesh=fine, in_specs=in_specs, out_specs=out_specs, check_vma=False)
```

```python
import functools
import math

import jax
import jax.numpy as jnp
from jax import lax
from jax.experimental import pallas as pl
from jax.experimental.pallas import tpu as pltpu
from jax.sharding import Mesh, PartitionSpec as P

HEADS = 16
HEAD_DIM = 64
D = HEADS * HEAD_DIM
TOK = 128
HALF = TOK // 2
N_CTX = 32
N_GRP = 4
N_X = 4
N_R = 8
SEQ = TOK * N_CTX
ID_ROWS = 16
IN_ROWS = TOK + HALF + ID_ROWS
OUT_ROWS = TOK + HALF
TQ = 256
LARGE, MIDDLE, SMALL = 2176, 896, 384
SUB = 128
Q_SRC = TQ // HALF
N_QB = N_CTX // Q_SRC
EPSILON = 1e-06
MASK = -1e30
MIB = 1024 * 1024
F32 = jnp.float32
BF16 = jnp.bfloat16


def dot_nn(a, b):
    return jnp.dot(a, b, preferred_element_type=F32)


def dot_nt(a, b):
    return lax.dot_general(a, b, (((1,), (1,)), ((), ())), preferred_element_type=F32)


def dot_tn(a, b):
    return lax.dot_general(a, b, (((0,), (0,)), ((), ())), preferred_element_type=F32)


def lanes(shape):
    return lax.broadcasted_iota(jnp.int32, shape, 1)


def fetch(wqkv_hbm, wo_hbm, wqkv, wo, sems, n, start):
    start = start if isinstance(start, int) else pl.multiple_of(start, 256)
    copies = [pltpu.make_async_copy(wo_hbm.at[pl.ds(start, 256), :], wo.at[n], sems.at[n, 3])]
    for m in range(3):
        cols = pl.ds(start + m * D, 256)
        copies.append(pltpu.make_async_copy(wqkv_hbm.at[:, cols], wqkv.at[n, m], sems.at[n, m]))
    return copies


FETCHED = [
    pltpu.VMEM((4, 3, D, 256), BF16),
    pltpu.VMEM((4, 256, D), BF16),
    pltpu.SemaphoreType.DMA((4, 4)),
]


def project_kernel(x_hbm, cot_hbm, gain_hbm, ids_hbm, wqkv_hbm, wo_hbm, send_ref, both_ref, x_ref, gain_ref, ids_ref, wqkv, wo, sems, in_sems):
    cot_ref = both_ref.at[:, D:]
    arrays = ((x_hbm, x_ref), (gain_hbm, gain_ref), (ids_hbm, ids_ref), (cot_hbm, cot_ref))
    inputs = [pltpu.make_async_copy(*pair, in_sems.at[n]) for n, pair in enumerate(arrays)]
    copies = [fetch(wqkv_hbm, wo_hbm, wqkv, wo, sems, n, n * 256) for n in range(4)]
    for copy in inputs + copies[0]:
        copy.start()
    for copy in inputs[:3]:
        copy.wait()
    for group in copies[1:]:
        for copy in group:
            copy.start()
    x = x_ref[...].astype(F32)
    cen = x - jnp.mean(x, axis=1, keepdims=True)
    inv = lax.rsqrt(jnp.mean(cen * cen, axis=1, keepdims=True) + EPSILON)
    n = (cen * inv * gain_ref[...]).astype(BF16)
    both_ref[:, :D] = n
    ids = ids_ref[...].astype(F32)
    rolled = jnp.concatenate([ids[:, HALF:], ids[:, :HALF]], axis=1)
    inputs[3].wait()
    for j in range(4):
        for copy in copies[j]:
            copy.wait()
        g = dot_nt(cot_ref[...], wo[j])
        q, k, v = (dot_nn(n, wqkv[j, m]) for m in range(3))
        for h in range(4):
            cols = slice(h * HEAD_DIM, (h + 1) * HEAD_DIM)
            kv = jnp.concatenate([k[:, cols], v[:, cols]], axis=1).astype(BF16)
            qg = jnp.concatenate([q[:, cols], g[:, cols]], axis=1).astype(BF16)
            for p in range(2):
                own = ids if p == 0 else rolled
                rows = jnp.concatenate(
                    [jnp.broadcast_to(ids, (8, TOK)), jnp.broadcast_to(own, (8, TOK))], axis=0
                )
                to = 8 * j + 2 * h + p
                send_ref[to, :TOK, :] = kv
                send_ref[to, TOK:OUT_ROWS, :] = qg[p * HALF:(p + 1) * HALF, :]
                send_ref[to, OUT_ROWS:, :] = rows.astype(BF16)


def project(x, cot, gain, ids, w_qkv, w_out):
    vmem = pl.BlockSpec(memory_space=pltpu.VMEM)
    hbm = pl.BlockSpec(memory_space=pltpu.HBM)
    return pl.pallas_call(
        project_kernel,
        in_specs=[hbm] * 6,
        out_specs=[vmem] * 2,
        out_shape=[
            jax.ShapeDtypeStruct((N_CTX, IN_ROWS, TOK), BF16),
            jax.ShapeDtypeStruct((TOK, 2 * D), BF16),
        ],
        scratch_shapes=[
            pltpu.VMEM((TOK, D), BF16),
            pltpu.VMEM((1, D), F32),
            pltpu.VMEM((1, TOK), jnp.int32),
            *FETCHED,
            pltpu.SemaphoreType.DMA((4,)),
        ],
        compiler_params=pltpu.CompilerParams(vmem_limit_bytes=56 * MIB),
        name="project",
    )(x, cot, gain, ids, w_qkv, w_out)


def attend_kernel(recv_ref, send_ref, kx, vx, kvt, idm, sc, acc):
    lane = lanes((TOK, TOK))
    feature = lane.astype(F32) - HEAD_DIM

    def prepare(c, largest):
        kv = recv_ref[c, :TOK, :].astype(F32)
        idrow = recv_ref[c, OUT_ROWS:, :].astype(F32)[:1]
        idm[pl.ds(c, 1), :] = idrow
        idcol = jnp.broadcast_to(idrow.astype(BF16), (TOK, TOK)).T.astype(F32)
        extra = jnp.where((feature == idcol) | ((feature > HEADS) & (feature < HEADS + 4)), 1.0, 0.0)
        rows = pl.ds(pl.multiple_of(c * TOK, TOK), TOK)
        kx[rows, :] = jnp.where(lane < HEAD_DIM, kv, extra).astype(BF16)
        vx[rows, :] = jnp.where(lane < HEAD_DIM, jnp.where(lane < 3, 1.0, 0.0), kv).astype(BF16)
        flipped = recv_ref[c, :TOK, :].T
        kvt[:TOK, rows] = flipped
        flipped = flipped.astype(F32)
        kvt[TOK:, rows] = jnp.ones((16, TOK), BF16)
        acc[rows, :] = jnp.zeros((TOK, TOK), F32)
        norm = jnp.sum(flipped[:HEAD_DIM] * flipped[:HEAD_DIM], axis=0, keepdims=True)
        return jnp.maximum(largest, norm)

    largest = lax.fori_loop(0, N_CTX, prepare, jnp.zeros((1, TOK), F32), unroll=8)
    key_norm = jnp.max(largest)
    for c in range(N_CTX, (SEQ + LARGE) // TOK):
        rows = slice(c * TOK, (c + 1) * TOK)
        kx[rows, :] = jnp.where(feature == HEADS, 1.0, 0.0).astype(BF16)
        vx[rows, :] = jnp.zeros((TOK, TOK), BF16)
        kvt[:, rows] = jnp.zeros((TOK + 16, TOK), BF16)

    lane_q = lanes((TQ, TOK))
    feature_q = lane_q.astype(F32) - HEAD_DIM
    row_t = lax.broadcasted_iota(jnp.int32, (TOK, TQ), 0)

    def three(row, start, rest):
        hi = row.astype(BF16).astype(F32)
        mid = (row - hi).astype(BF16).astype(F32)
        low = row - hi - mid
        for n, part in enumerate((hi, mid, low)):
            rest = jnp.where(row_t == start + n, part, rest)
        return rest.astype(BF16)

    def query_block(i, carry):
        c0 = i * Q_SRC
        qd = recv_ref[pl.ds(c0, Q_SRC), TOK:OUT_ROWS, :].reshape(TQ, TOK).astype(F32)
        idcols = []
        lowest, highest = None, None
        for a in range(Q_SRC):
            both = recv_ref[c0 + a, OUT_ROWS:, :].astype(F32)
            idcols.append(jnp.broadcast_to(both[8:9].astype(BF16), (TOK, TOK)).T[:HALF].astype(F32))
            lowest = both if lowest is None else jnp.minimum(lowest, both)
            highest = both if highest is None else jnp.maximum(highest, both)
        idcol = jnp.concatenate(idcols, axis=0)
        every = idm[...]
        below = jnp.sum(jnp.where(every < jnp.min(lowest), 1.0, 0.0)).astype(jnp.int32)
        upto = jnp.sum(jnp.where(every <= jnp.max(highest), 1.0, 0.0)).astype(jnp.int32)
        start = below // TOK
        extent = upto - start * TOK
        n_large = (extent + (LARGE - 1 - MIDDLE - SMALL)) // LARGE
        extent = jnp.maximum(extent - n_large * LARGE, 0)
        n_middle = (extent + (MIDDLE - 1 - SMALL)) // MIDDLE
        n_small = (jnp.maximum(extent - n_middle * MIDDLE, 0) + (SMALL - 1)) // SMALL

        qdt = qd.astype(BF16).T.astype(F32)
        other = jnp.where((feature_q != idcol) & (feature_q < HEADS + 1), MASK, 0.0)
        qxt_f = jnp.where(lane_q < HEAD_DIM, qd * 0.125, other).astype(BF16).T.astype(F32)
        norms = jnp.sum(qxt_f[:HEAD_DIM] * qxt_f[:HEAD_DIM], axis=0, keepdims=True)
        small = jnp.max(norms) * key_norm < 1600.0

        def steps(step, state, wanted=True):
            def run(first, size):
                def body(n, state):
                    base = first + n * size
                    return step(
                        [
                            pl.ds(pl.multiple_of(base + t * SUB, TOK), SUB)
                            for t in range(size // SUB)
                        ],
                        state,
                    )

                return body

            first = start * TOK
            for size, count in ((LARGE, n_large), (MIDDLE, n_middle), (SMALL, n_small)):
                state = lax.fori_loop(0, jnp.where(wanted, count, 0), run(first, size), state)
                first = first + count * size
            return state

        def largest_step(tiles, top):
            for rows in tiles:
                s = dot_nn(kx[rows, :], qxt_f.astype(BF16))
                for r in range(0, SUB, 8):
                    top = jnp.maximum(top, s[r:r + 8])
            return top

        top = steps(largest_step, jnp.full((8, TQ), MASK, F32), ~small)
        top = jnp.where(small, 0.0, jnp.max(top, axis=0, keepdims=True))
        qxt = three(-top, HEAD_DIM + HEADS + 1, qxt_f)

        def value_step(tiles, ot):
            e = [jnp.exp(dot_nn(kx[rows, :], qxt)).astype(BF16) for rows in tiles]
            for n in range(0, len(tiles), 2):
                k = min(2, len(tiles) - n)
                rows = pl.ds(pl.multiple_of(tiles[n].start, TOK), k * SUB)
                ot = ot + dot_nn(kvt[HEAD_DIM:, rows], jnp.concatenate(e[n:n + k], axis=0))
            for rows, part in zip(tiles, e):
                sc[rows, :] = part
            return ot

        ot = steps(value_step, jnp.zeros((HEAD_DIM + 16, TQ), F32))
        inv = 1.0 / ot[HEAD_DIM:HEAD_DIM + 1]
        ot = (ot[:HEAD_DIM] * inv).astype(BF16).astype(F32)
        delta = jnp.sum(ot * qdt[HEAD_DIM:], axis=0, keepdims=True)
        gxt = three(-delta, 0, jnp.where(row_t < HEAD_DIM, 0.0, qdt))

        scaled = (qdt * inv).T
        right = jnp.concatenate(
            [
                jnp.where(lane_q < HEAD_DIM, scaled * 0.125, 0.0).astype(BF16),
                jnp.where(lane_q >= HEAD_DIM, scaled, 0.0).astype(BF16),
            ],
            axis=0,
        )

        def grad_step(tiles, dqt):
            e = [sc[rows, :] for rows in tiles]
            ds = [part * dot_nn(vx[rows, :], gxt).astype(BF16) for rows, part in zip(tiles, e)]
            for n in range(0, len(tiles), 2):
                k = min(2, len(tiles) - n)
                rows = pl.ds(pl.multiple_of(tiles[n].start, TOK), k * SUB)
                dqt = dqt + dot_nn(kvt[:HEAD_DIM, rows], jnp.concatenate(ds[n:n + k], axis=0))
            added = [
                part
                for n in range(0, len(tiles), 3)
                for k in [min(3, len(tiles) - n)]
                for big in [dot_nn(jnp.concatenate([jnp.concatenate(ds[n:n + k], axis=0), jnp.concatenate(e[n:n + k], axis=0)], axis=1), right)]
                for t in range(k)
                for part in [acc[tiles[n + t], :] + big[t * SUB:(t + 1) * SUB]]
            ]
            for rows, part in zip(tiles, added):
                acc[rows, :] = part
            return dqt

        dqt = steps(grad_step, jnp.zeros((HEAD_DIM, TQ), F32))
        both = jnp.concatenate([ot, dqt * (inv * 0.125)], axis=0).T.astype(BF16)
        for a in range(Q_SRC):
            send_ref[(c0 + a) % N_R, (c0 + a) // N_R, TOK:, :] = both[a * HALF:(a + 1) * HALF]
        return carry

    lax.fori_loop(0, N_QB, query_block, 0)

    def finish(c, carry):
        rows = pl.ds(pl.multiple_of(c * TOK, TOK), TOK)
        send_ref[c % N_R, c // N_R, :TOK, :] = acc[rows, :].astype(BF16)
        return carry

    lax.fori_loop(0, N_CTX, finish, 0, unroll=8)


def attend(recv):
    vmem = pl.BlockSpec(memory_space=pltpu.VMEM)
    padded = SEQ + LARGE
    return pl.pallas_call(
        attend_kernel,
        in_specs=[vmem],
        out_specs=vmem,
        out_shape=jax.ShapeDtypeStruct((N_R, N_X, OUT_ROWS, TOK), BF16),
        scratch_shapes=[
            pltpu.VMEM((padded, TOK), BF16),
            pltpu.VMEM((padded, TOK), BF16),
            pltpu.VMEM((TOK + 16, padded), BF16),
            pltpu.VMEM((N_CTX, TOK), F32),
            pltpu.VMEM((padded, TQ), BF16),
            pltpu.VMEM((padded, TOK), F32),
        ],
        compiler_params=pltpu.CompilerParams(vmem_limit_bytes=28 * MIB),
        cost_estimate=pl.CostEstimate(flops=25 * 10**9, bytes_accessed=4 * 10**6, transcendentals=0),
        name="attend",
    )(recv)


def unproject_kernel(me_ref, c0, c1, c2, c3, x_hbm, gain_hbm, wqkv_hbm, wo_hbm, out_ref, gx_ref, x_ref, gain_ref, wqkv, wo, sems, in_sems):
    copies = [
        fetch(wqkv_hbm, wo_hbm, wqkv, wo, sems, d, (me_ref[0] ^ d) * 256) for d in range(N_X)
    ]
    for group in copies:
        for copy in group:
            copy.start()
    inputs = [
        pltpu.make_async_copy(x_hbm, x_ref, in_sems.at[0]),
        pltpu.make_async_copy(gain_hbm, gain_ref, in_sems.at[1]),
    ]
    for copy in inputs:
        copy.start()
    result = jnp.zeros((TOK, D), F32)
    g = jnp.zeros((TOK, D), F32)
    for d, ref in enumerate((c0, c1, c2, c3)):
        for copy in copies[d]:
            copy.wait()
        result = result + dot_nn(ref[:, 768:], wo[d])
        for m in range(3):
            g = g + dot_nt(ref[:, m * 256:(m + 1) * 256], wqkv[d, m])
    out_ref[...] = result.astype(BF16)
    for copy in inputs:
        copy.wait()
    x = x_ref[...].astype(F32)
    cen = x - jnp.mean(x, axis=1, keepdims=True)
    inv = lax.rsqrt(jnp.mean(cen * cen, axis=1, keepdims=True) + EPSILON)
    x_hat = cen * inv
    g = g * gain_ref[...]
    gx = inv * (
        g - jnp.mean(g, axis=1, keepdims=True) - x_hat * jnp.mean(g * x_hat, axis=1, keepdims=True)
    )
    gx_ref[...] = gx.astype(BF16)


def unproject(me, pieces, x, gain, w_qkv, w_out):
    vmem = pl.BlockSpec(memory_space=pltpu.VMEM)
    hbm = pl.BlockSpec(memory_space=pltpu.HBM)
    return pl.pallas_call(
        unproject_kernel,
        in_specs=[pl.BlockSpec(memory_space=pltpu.SMEM)] + [vmem] * 4 + [hbm] * 4,
        out_specs=[vmem] * 2,
        out_shape=[jax.ShapeDtypeStruct((TOK, D), BF16)] * 2,
        scratch_shapes=[
            pltpu.VMEM((TOK, D), BF16),
            pltpu.VMEM((1, D), F32),
            *FETCHED,
            pltpu.SemaphoreType.DMA((2,)),
        ],
        compiler_params=pltpu.CompilerParams(vmem_limit_bytes=52 * MIB),
        cost_estimate=pl.CostEstimate(flops=7 * 10**9, bytes_accessed=10**7, transcendentals=0),
        name="unproject",
    )(me, *pieces, x, gain, w_qkv, w_out)


def repack_kernel(me_ref, recv_ref, *cols_refs):
    for d, cols_ref in enumerate(cols_refs):
        at = me_ref[0] ^ d
        parts = [[], [], [], []]
        for h in range(4):
            lo, hi = recv_ref[2 * h, at].astype(F32), recv_ref[2 * h + 1, at].astype(F32)
            kv = lo[:TOK] + hi[:TOK]
            aq = jnp.concatenate([lo[TOK:], hi[TOK:]], axis=0)
            parts[0].append(aq[:, HEAD_DIM:])
            parts[1].append(kv[:, :HEAD_DIM])
            parts[2].append(kv[:, HEAD_DIM:])
            parts[3].append(aq[:, :HEAD_DIM])
        for n, part in enumerate(parts):
            cols_ref[:, n * 256:(n + 1) * 256] = jnp.concatenate(part, axis=1).astype(BF16)


def repack(me, recv):
    vmem = pl.BlockSpec(memory_space=pltpu.VMEM)
    return pl.pallas_call(
        repack_kernel,
        in_specs=[pl.BlockSpec(memory_space=pltpu.SMEM), vmem],
        out_specs=[vmem] * N_X,
        out_shape=[jax.ShapeDtypeStruct((TOK, D), BF16)] * N_X,
        compiler_params=pltpu.CompilerParams(vmem_limit_bytes=16 * MIB),
        name="repack",
    )(me, recv)


def weights_kernel(me_ref, c0, c1, c2, c3, b0, b1, b2, b3, own_ref, other_ref):
    cols_refs = (c0, c1, c2, c3)
    cols = jnp.concatenate([ref[...] for ref in cols_refs], axis=0)
    both = jnp.concatenate([b0[...], b1[...], b2[...], b3[...]], axis=0)
    first_core = me_ref[1] == 0
    for zl in range(2):
        parts = []
        for m in (2 * zl, 2 * zl + 1):
            left = dot_tn(both[:, m * 256:(m + 1) * 256], cols[:, :768])
            right = dot_tn(cols[:, 768:], both[:, D + m * 256:D + (m + 1) * 256])
            parts.append((left, right))
        for n in range(2):
            cols_of = slice(0, 768) if n == 0 else slice(768, D)
            own = jnp.where(first_core, parts[0][n], parts[1][n]).astype(BF16)
            other = jnp.where(first_core, parts[1][n], parts[0][n]).astype(BF16)
            for r in range(N_R):
                own_ref[8 * zl + r, :, cols_of] = own[32 * r:32 * r + 32]
                other_ref[8 * zl + r, :, cols_of] = other[32 * r:32 * r + 32]


def weights(me, cols, both):
    vmem = pl.BlockSpec(memory_space=pltpu.VMEM)
    return pl.pallas_call(
        weights_kernel,
        in_specs=[pl.BlockSpec(memory_space=pltpu.SMEM)] + [vmem] * 8,
        out_specs=[vmem] * 2,
        out_shape=[jax.ShapeDtypeStruct((N_CTX // 2, 32, D), BF16)] * 2,
        cost_estimate=pl.CostEstimate(flops=2 * 10**9, bytes_accessed=4 * 10**6, transcendentals=0),
        compiler_params=pltpu.CompilerParams(vmem_limit_bytes=24 * MIB),
        name="weights",
    )(me, *cols, *both)


def assemble_kernel(me_ref, a_ref, b_ref, c_ref, d_ref, qkv_ref, out_ref):
    for d, ref in enumerate((a_ref, b_ref, c_ref, d_ref)):
        start = (me_ref[0] ^ d) * 256
        part = ref[...].astype(F32)
        for n in range(3):
            cols = pl.ds(pl.multiple_of(start + n * D, 256), 256)
            qkv_ref[:, cols] = part[:, n * 256:(n + 1) * 256]
        out_ref[:, pl.ds(pl.multiple_of(start, 256), 256)] = part[:, 768:]


def assemble(me, parts):
    vmem = pl.BlockSpec(memory_space=pltpu.VMEM)
    return pl.pallas_call(
        assemble_kernel,
        in_specs=[pl.BlockSpec(memory_space=pltpu.SMEM)] + [vmem] * 4,
        out_specs=[vmem] * 2,
        out_shape=[jax.ShapeDtypeStruct((32, 3 * D), F32), jax.ShapeDtypeStruct((32, D), F32)],
        compiler_params=pltpu.CompilerParams(vmem_limit_bytes=8 * MIB),
        name="assemble",
    )(me, *parts)


def swap(piece, axis, d):
    return piece if d == 0 else lax.ppermute(piece, axis, [(i, i ^ d) for i in range(4)])


def shards(patches, gain, w_qkv, w_out, image_ids, grad_out):
    x, cot = patches[0], grad_out[0]
    gain_row = gain[None]
    me = jnp.stack([lax.axis_index("x"), lax.axis_index("core")]).astype(jnp.int32)
    me_grp = lax.axis_index(("zl", "core")).astype(jnp.int32)[None]
    send, both = project(x, cot, gain_row, image_ids, w_qkv, w_out)
    recv = lax.all_to_all(send, ("x", "r"), 0, 0, tiled=True)
    recv, both = lax.optimization_barrier((recv, both))
    both = [swap(both, "x", d) for d in range(N_X)]
    done, both, me, me_grp = lax.optimization_barrier((attend(recv), both, me, me_grp))
    back = lax.all_to_all(done, "r", 0, 0, tiled=True)
    cols = repack(me, back)
    own, other = weights(me, cols, both)
    got = lax.ppermute(other, "core", [(0, 1), (1, 0)])
    cols = [swap(cols[d], "x", d) for d in range(N_X)]
    terms = (own.astype(F32) + got.astype(F32)).astype(BF16)
    parts = lax.all_to_all(terms, ("zl", "r"), 0, 0, tiled=True)
    out, grad_x = unproject(me, cols, x, gain_row, w_qkv, w_out)
    factor = 1.0 / math.sqrt(N_GRP * SEQ)
    share = (jnp.sum(parts.astype(F32), axis=0) * factor).astype(BF16)
    flip = [(s * N_X + j, j * N_X + s) for s in range(N_GRP) for j in range(N_X)]
    share_qkv = lax.ppermute(share[:, :768], ("zl", "core", "x"), flip)
    share = jnp.concatenate([share_qkv, share[:, 768:]], axis=1)
    shares = [swap(share, ("zl", "core"), d) for d in range(N_GRP)]
    grad_qkv, grad_w_out = assemble(me_grp, shares)
    return out[None], grad_x[None], grad_qkv, grad_w_out


def solution(mesh):
    fine = Mesh(mesh.devices.reshape(2, 2, N_X, N_R), ("zl", "core", "x", "r"))
    grp, ctx = ("zl", "core"), ("x", "r")
    in_specs = (P(grp, ctx, None), P(), P(), P(), P(grp, ctx), P(grp, ctx, None))
    out_specs = (P(grp, ctx, None), P(grp, ctx, None), P(ctx, None), P(ctx, None))
    return jax.shard_map(shards, mesh=fine, in_specs=in_specs, out_specs=out_specs, check_vma=False)
```
